512 devices in a mesh: blk: 256 (over y, x, z_hi, core), pr: 2 (over z_lo).
Axes of the slice: x: 4, y: 8, z: 8 (z_hi: 4, z_lo: 2; z = z_hi * 2 + z_lo), core: 2. Of those that a mesh axis runs over, the one named last changes fastest.
Arguments:
- coords: float32 [3, 524288], P(None, 'blk'), may hold values from -4 to 4
- probes: float32 [64, 524288], P('pr', 'blk'), may hold values from -6 to 6
- solves: float32 [64, 524288], P(None, 'blk'), may hold values from -6 to 6
- alpha: float32 [524288], P('blk'), may hold values from -6 to 6
- lengthscale: float32 [1], replicated, may hold values from 0.6 to 1.6
- column_pick: int32 [64], replicated, may hold values from 0 to 63, as said below
- plan: int32 [3, 256], replicated, may hold values from 0 to 255, as said below
Outputs:
- kernel_probes: float32 [64, 524288], P('pr', 'blk')
- slope_probes: float32 [64, 524288], P('pr', 'blk')
- gradients: float32 [2], replicated
The draws below stay inside these ranges and needn't reach their ends.
Inputs may be any that keep to these rules, and one draw needn't show every extreme that they name: Row r of plan is block index xor s_r for a round value s_r of 1 to 255, distinct over rows; 256 is a power of two. `column_pick`: A permutation of 0 to 63.
All inputs are finite; a program needn't handle non-finite values.
Results may differ from the reference program's by a relative error of at most 0.00012.
Values sent between devices are 32-bit elements; how exact they have to be, the bound alone decides.
A program may use at most 128 MiB of HBM per device.

```python
import math
import jax
import jax.numpy as jnp
from jax import lax

BLOCK = 2048
PROBES = 64
ROUNDS = 3
NBLK = 256
NPTS = 524288


def shared_parts(key):
    base = jax.random.normal(jax.random.fold_in(key, 101), (PROBES, NPTS), jnp.float32)
    base = jnp.clip(base, -6.0, 6.0)
    order = jax.random.permutation(jax.random.fold_in(key, 102), PROBES).astype(jnp.int32)
    return (base, order)


def draw_probes(key, part):
    base, order = shared_parts(key)
    return base


def draw_column_pick(key, part):
    base, order = shared_parts(key)
    return order.astype(jnp.int32)


def draw_solves(key, part):
    base, order = shared_parts(key)
    key = jax.random.fold_in(key, 7)
    coupling = 0.5
    noise = 0.8 * jax.random.normal(key, (PROBES, NPTS), jnp.float32)
    mixed = coupling * base + noise
    stored = jnp.zeros((PROBES, NPTS), jnp.float32).at[order].set(mixed)
    return jnp.clip(stored, -6.0, 6.0)


def draw_plan(key, part):
    key = jax.random.fold_in(key, 11)
    values = jax.random.permutation(key, NBLK - 1)[:ROUNDS] + 1
    blocks = jnp.arange(NBLK, dtype=jnp.int32)
    return jnp.bitwise_xor(blocks[None, :], values.astype(jnp.int32)[:, None]).astype(jnp.int32)


def levels(rng, dims, shards, smallest, high):
    gain = 1.0
    for position, blocks in shards:
        steps = jax.random.uniform(jax.random.fold_in(jax.random.fold_in(rng, 6), position), (blocks,), jnp.float32, smallest / len(shards), high / len(shards))
        gain = gain * jnp.repeat(jnp.exp(steps), dims[position] // blocks).reshape((-1,) + (1,) * (len(dims) - 1 - position))
    return gain


def normal_values(stream_key, dims, scale, most, shards=(), kind=jnp.bfloat16):
    entries = jax.random.normal(stream_key, dims, jnp.float32) * scale
    if len(shards) > 0:
        entries = levels(stream_key, dims, shards, -0.22, 0.18) * entries
    return jnp.clip(entries, min=-most, max=most).astype(kind)


def setup_inputs(seed: int = 0) -> dict:
    streams_of = jax.random.split(jax.random.key(seed), 8)
    coords = normal_values(streams_of[0], (3, NPTS), 1.0, 4.0, ((1, 256),), jnp.float32)
    probes = draw_probes(jax.random.fold_in(streams_of[7], 71), 0)
    solves = draw_solves(jax.random.fold_in(streams_of[7], 71), 0)
    alpha = normal_values(streams_of[3], (NPTS,), 1.0, 6.0, ((0, 256),), jnp.float32)
    lengthscale = jnp.clip(jnp.exp(jax.random.uniform(streams_of[4], (1,), jnp.float32, math.log(0.6), math.log(1.6))), 0.6, 1.6)
    column_pick = draw_column_pick(jax.random.fold_in(streams_of[7], 71), 0)
    plan = draw_plan(jax.random.fold_in(streams_of[7], 71), 0)
    return dict(coords=coords, probes=probes, solves=solves, alpha=alpha, lengthscale=lengthscale, column_pick=column_pick, plan=plan)


def tile_terms(rows_x, cols_x, scale_len):
    dist_sq = jnp.zeros((rows_x.shape[1], cols_x.shape[1]), jnp.float32)
    for component in range(3):
        offset = rows_x[component][:, None] - cols_x[component][None, :]
        dist_sq = dist_sq + offset * offset
    scaled = jnp.sqrt(5.0 * dist_sq) / scale_len
    decay = jnp.exp(-scaled)
    kernel = (1.0 + scaled + scaled * scaled / 3.0) * decay
    slope = scaled * scaled / (3.0 * scale_len) * (1.0 + scaled) * decay
    return (kernel, slope)

def hdot(left, right):
    return jnp.dot(left, right, precision=lax.Precision.HIGHEST, preferred_element_type=jnp.float32)

def reference(coords, probes, solves, alpha, lengthscale, column_pick, plan):
    scale_len = lengthscale[0]
    coord_blocks = coords.reshape(3, NBLK, BLOCK).transpose(1, 0, 2)
    probe_blocks = probes.reshape(PROBES, NBLK, BLOCK).transpose(1, 0, 2)
    alpha_blocks = alpha.reshape(NBLK, BLOCK)
    kernel_probes = jnp.zeros((NBLK, PROBES, BLOCK), jnp.float32)
    slope_probes = jnp.zeros((NBLK, PROBES, BLOCK), jnp.float32)
    quad = jnp.float32(0.0)
    for round_no in range(ROUNDS):
        partners = plan[round_no]

        def one_block(block_no):
            mate = partners[block_no]
            kernel, slope = tile_terms(coord_blocks[mate], coord_blocks[block_no], scale_len)
            kz_part = hdot(probe_blocks[mate], kernel)
            dkz_part = hdot(probe_blocks[mate], slope)
            quad_part = jnp.sum(hdot(alpha_blocks[mate], slope) * alpha_blocks[block_no])
            return (kz_part, dkz_part, quad_part)
        kz_round, dkz_round, quad_round = lax.map(one_block, jnp.arange(NBLK, dtype=jnp.int32))
        kernel_probes = kernel_probes + kz_round
        slope_probes = slope_probes + dkz_round
        quad = quad + jnp.sum(quad_round)
    kernel_probes = kernel_probes.transpose(1, 0, 2).reshape(PROBES, NPTS)
    slope_probes = slope_probes.transpose(1, 0, 2).reshape(PROBES, NPTS)
    picked = solves[column_pick, :]
    trace_noise = jnp.sum(picked * probes)
    trace_slope = jnp.sum(picked * slope_probes)
    grad_noise = 0.5 * (jnp.sum(alpha * alpha) - trace_noise / PROBES) / BLOCK
    grad_len = 0.5 * (quad - trace_slope / PROBES) / BLOCK
    return (kernel_probes, slope_probes, jnp.stack([grad_noise, grad_len]).astype(jnp.float32))
```

```python
import math
import jax
import jax.numpy as jnp
from jax import lax
from jax.experimental import pallas as pl
from jax.experimental.pallas import tpu as pltpu
from jax.sharding import PartitionSpec as P

F32, BF16 = jnp.float32, jnp.bfloat16
MESH = pl.DeviceIdType.MESH
ROUNDS = 3
COLS = 2048
HALF = 1024
TB = 512
TA = 256
STRIP = 16


def split(value):
    hi = value.astype(BF16)
    return hi, (value - hi.astype(F32)).astype(BF16)


def tile_terms(xa, xb, ka, kb, k2):
    d2 = None
    for comp in range(3):
        off = xa[:, comp:comp + 1] - xb[comp]
        d2 = off * off if d2 is None else d2 + off * off
    dist = d2 * lax.rsqrt(jnp.maximum(d2, 1e-30))
    decay = jnp.exp2(dist * ka)
    bell = (1.0 + dist * kb) * decay
    return bell + (d2 * k2) * decay, d2 * bell


def whole(ref, sem):
    pltpu.make_async_copy(ref, ref, sem).wait()


def body(
    plan, pick, cst, coords, alpha, probes, solves,
    kz_out, dkz_out, grad_out,
    comps, buf_a, buf_ac, st_a, st_ac, buf_b, buf_bc, buf_c0, buf_c1, buf_c2, buf_cc, st_b, st_bc, p32, payc,
    picked, plhs, xat, khi, klo, shi, slo, acc_k, acc_s, buf_r, sc1, buf_s1, sc2, buf_s2,
    s_a1, r_a1, s_a2, r_a2, s_b1, r_b1, s_b2, r_b2, s_r, r_r, s_s, r_s,
):
    buf_c = (buf_c0, buf_c1, buf_c2)
    blk = lax.axis_index("blk")
    half = lax.axis_index("pr")
    core = blk % 2
    zhi = (blk // 2) % 4
    x = (blk // 8) % 4
    y = blk // 32
    m_a = y * 4 + zhi
    m_b = x * 2 + core
    a64 = half * 32 + m_a

    def dev_a(k):
        m = k % 32
        return {"blk": (((m // 4) * 4 + x) * 4 + m % 4) * 2 + core, "pr": k // 32}

    def dev_b(k):
        return {"blk": ((y * 4 + k // 2) * 4 + zhi) * 2 + k % 2, "pr": half}

    def send(src, dst, ssem, rsem, dev):
        pltpu.make_async_remote_copy(
            src_ref=src, dst_ref=dst, send_sem=ssem, recv_sem=rsem, device_id=dev, device_id_type=MESH
        ).start()

    shifts = [plan[r, 0] for r in range(ROUNDS)]
    t_a = [(s // 32) * 4 + (s // 2) % 4 for s in shifts]
    t_b = [((s // 8) % 4) * 2 + s % 2 for s in shifts]

    barrier = pltpu.get_barrier_semaphore()

    def greet_a(k, _):
        pl.semaphore_signal(barrier, inc=1, device_id=dev_a((a64 + k) % 64), device_id_type=MESH)
        return 0

    def greet_b(k, _):
        pl.semaphore_signal(barrier, inc=1, device_id=dev_b((m_b + k) % 8), device_id_type=MESH)
        return 0

    lax.fori_loop(1, 64, greet_a, 0)
    lax.fori_loop(1, 8, greet_b, 0)

    for g in range(4):
        row = coords[g:g + 1, :] if g < 3 else alpha[...]
        for t in range(16):
            comps[g, t] = row[:, t * 128:(t + 1) * 128]
    pl.semaphore_wait(barrier, 70)

    def probe_tile(hh, yy, zz):
        rows = pl.ds(pl.multiple_of(zz * 8, 8), 8)
        return rows, pl.ds(pl.multiple_of(hh * HALF + yy * 128, 128), 128)

    def spread_comps(k, _):
        m = (m_a + k) % 32
        send(comps.at[m % 4, half * 8 + m // 4], buf_ac.at[m_a], s_a1.at[0], r_a1.at[0], dev_a(half * 32 + m))
        return 0

    def spread_probes(k, _):
        d = (a64 + k) % 64
        m = d % 32
        rows, cols = probe_tile(d // 32, m // 4, m % 4)
        send(probes.at[rows, cols], buf_a.at[a64], s_a1.at[1], r_a1.at[1], dev_a(d))
        return 0

    lax.fori_loop(1, 32, spread_comps, 0)
    lax.fori_loop(1, 64, spread_probes, 0)
    buf_ac[m_a] = comps[zhi, half * 8 + y]
    rows, cols = probe_tile(half, y, zhi)
    buf_a[a64] = probes[rows, cols]

    for j in range(64):
        picked[j:j + 1, :] = solves[pl.ds(pick[j], 1), :]

    whole(buf_ac.at[0:31], r_a1.at[0])

    def select_ac(k, _):
        i = (m_a + k) % 32
        for r in range(ROUNDS):
            st_ac[i, r:r + 1, :] = buf_ac[i ^ t_a[r]]
        st_ac[i, 3:4, :] = jnp.zeros((1, 128), F32)
        send(st_ac.at[i], buf_bc.at[y, zhi], s_a2.at[3], r_a2.at[3], dev_a(half * 32 + i))
        return 0

    lax.fori_loop(1, 32, select_ac, 0)
    for r in range(ROUNDS):
        buf_bc[y, zhi, r:r + 1, :] = buf_ac[m_a ^ t_a[r]]
    buf_bc[y, zhi, 3:4, :] = jnp.zeros((1, 128), F32)

    whole(buf_a.at[0:63], r_a1.at[1])

    def select_a(r):
        def one(k, _):
            i = (m_a + k) % 32
            j = i ^ t_a[r]
            st_a[r, i, 0] = buf_a[j]
            st_a[r, i, 1] = buf_a[32 + j]
            send(st_a.at[r, i], buf_b.at[r, y, zhi], s_a2.at[r], r_a2.at[r], dev_a(half * 32 + i))
            return 0

        lax.fori_loop(1, 32, one, 0)
        j = m_a ^ t_a[r]
        buf_b[r, y, zhi, 0] = buf_a[j]
        buf_b[r, y, zhi, 1] = buf_a[32 + j]

    def spread_b(r):
        whole(st_a.at[r, 0:31], r_a2.at[r])

        def one(k, _):
            d = (m_b + k) % 8
            send(buf_b.at[r, d], buf_c[r].at[m_b], s_b1.at[r], r_b1.at[r], dev_b(d))
            return 0

        lax.fori_loop(1, 8, one, 0)
        buf_c[r][m_b] = buf_b[r, m_b]

    def select_b(r):
        whole(buf_c[r].at[0:7], r_b1.at[r])
        cols = pl.ds(pl.multiple_of(m_b * 128, 128), 128)

        def one(k, _):
            d = (m_b + k) % 8
            j = d ^ t_b[r]
            for hh in range(2):
                for g in range(4):
                    lo = (hh * 4 + g) * 8
                    st_b[r, d, lo:lo + 8, :] = buf_c[r][j, g, hh]
            send(st_b.at[r, d], p32.at[r, 0:64, cols], s_b2.at[r], r_b2.at[r], dev_b(d))
            return 0

        lax.fori_loop(1, 8, one, 0)
        j = m_b ^ t_b[r]
        for hh in range(2):
            for g in range(4):
                lo = (hh * 4 + g) * 8
                p32[r, lo:lo + 8, cols] = buf_c[r][j, g, hh]

    for r in range(ROUNDS):
        select_a(r)

    whole(st_ac.at[0:31], r_a2.at[3])

    def spread_bc(k, _):
        d = (m_b + k) % 8
        send(buf_bc.at[d], buf_cc.at[m_b], s_b1.at[3], r_b1.at[3], dev_b(d))
        return 0

    lax.fori_loop(1, 8, spread_bc, 0)
    buf_cc[m_b] = buf_bc[m_b]
    whole(buf_cc.at[0:7], r_b1.at[3])

    def select_bc(k, _):
        d = (m_b + k) % 8
        for r in range(ROUNDS):
            for g in range(4):
                st_bc[d, g, r:r + 1, :] = buf_cc[d ^ t_b[r], g, r:r + 1, :]
        for g in range(4):
            st_bc[d, g, 3:4, :] = jnp.zeros((1, 128), F32)
        send(st_bc.at[d], payc.at[m_b], s_b2.at[3], r_b2.at[3], dev_b(d))
        return 0

    lax.fori_loop(1, 8, select_bc, 0)
    for r in range(ROUNDS):
        for g in range(4):
            payc[m_b, g, r:r + 1, :] = buf_cc[m_b ^ t_b[r], g, r:r + 1, :]
    for r in range(ROUNDS):
        spread_b(r)
    whole(st_bc.at[0:7], r_b2.at[3])
    for r in range(ROUNDS):
        for t in range(8):
            for g in range(4):
                p32[r, 64 + g:65 + g, t * 128:(t + 1) * 128] = payc[t, g, r:r + 1, :]
        p32[r, 68:72, :] = jnp.zeros((4, HALF), F32)
    for r in range(ROUNDS):
        select_b(r)

    acc_k[...] = jnp.zeros_like(acc_k)
    acc_s[...] = jnp.zeros_like(acc_s)
    noise = jnp.sum(
        picked[pl.ds(pl.multiple_of(half * 32, 32), 32), :] * probes[...], axis=0, keepdims=True
    )
    own = alpha[...]
    noise = 0.5 * own * own - noise * (1.0 / 64.0)

    ka, kb, k2, k_slope = cst[0], cst[1], cst[2], cst[3]

    for r in range(ROUNDS):
        whole(st_b.at[r, 0:7], r_b2.at[r])
        p = jnp.concatenate([p32[r], jnp.zeros((8, HALF), F32)], 0)
        hi, lo = split(p)
        plhs[0:80, :] = hi
        plhs[80:160, :] = lo
        xat[...] = jnp.transpose(p32[r, 64:72, :])

        def step(t, _):
            b = pl.multiple_of(t * TB, TB)
            xb = [coords[c:c + 1, pl.ds(b, TB)] for c in range(3)]
            sum_k = sum_s = None
            for a in range(0, HALF, TA):
                for st in range(a, a + TA, STRIP):
                    kern, slope = tile_terms(xat[st:st + STRIP, :], xb, ka, kb, k2)
                    khi[st:st + STRIP, :], klo[st:st + STRIP, :] = split(kern)
                    shi[st:st + STRIP, :], slo[st:st + STRIP, :] = split(slope)
                lhs = plhs[:, a:a + TA]

                def product(hi, lo):
                    one = jnp.dot(lhs, hi[a:a + TA, :], preferred_element_type=F32)
                    two = jnp.dot(lhs[:80], lo[a:a + TA, :], preferred_element_type=F32)
                    return one[:72] + one[80:152] + two[:72]

                more_k, more_s = product(khi, klo), product(shi, slo)
                sum_k = more_k if sum_k is None else sum_k + more_k
                sum_s = more_s if sum_s is None else sum_s + more_s
            acc_k[:, pl.ds(b, TB)] += sum_k
            acc_s[:, pl.ds(b, TB)] += sum_s
            return 0

        lax.fori_loop(0, COLS // TB, step, 0)

    other = pl.ds(pl.multiple_of((1 - half) * 32, 32), 32)
    mine = pl.ds(pl.multiple_of(half * 32, 32), 32)
    mate = {"blk": blk, "pr": 1 - half}
    send(acc_k.at[other, :], buf_r.at[0], s_r.at[0], r_r.at[0], mate)
    send(acc_s.at[other, :], buf_r.at[1], s_r.at[1], r_r.at[1], mate)

    slope = acc_s[67:68, :] * own - jnp.sum(picked[...] * acc_s[0:64, :], axis=0, keepdims=True) * (1.0 / 64.0)
    slope = slope * k_slope
    rows_n, rows_s = noise[:, 0:128], slope[:, 0:128]
    for t in range(1, 16):
        rows_n = rows_n + noise[:, t * 128:(t + 1) * 128]
        rows_s = rows_s + slope[:, t * 128:(t + 1) * 128]
    sc1[0:1, :] = rows_n
    sc1[1:2, :] = rows_s

    def scalars_a(k, _):
        send(sc1, buf_s1.at[a64], s_s.at[0], r_s.at[0], dev_a((a64 + k) % 64))
        return 0

    lax.fori_loop(1, 64, scalars_a, 0)
    buf_s1[a64] = sc1[...]
    whole(buf_s1.at[0:63], r_s.at[0])
    sc2[...] = jnp.sum(buf_s1[...], axis=0)

    def scalars_b(k, _):
        send(sc2, buf_s2.at[m_b], s_s.at[1], r_s.at[1], dev_b((m_b + k) % 8))
        return 0

    lax.fori_loop(1, 8, scalars_b, 0)
    buf_s2[m_b] = sc2[...]

    whole(buf_r.at[0], r_r.at[0])
    kz_out[...] = acc_k[mine, :] + buf_r[0]
    whole(buf_r.at[1], r_r.at[1])
    dkz_out[...] = (acc_s[mine, :] + buf_r[1]) * k_slope

    whole(buf_s2.at[0:7], r_s.at[1])
    total = jnp.sum(jnp.sum(buf_s2[...], axis=0), axis=1, keepdims=True) * (0.5 / COLS)
    grad_out[...] = jnp.broadcast_to(total, (2, 128))

    whole(buf_ac.at[0:31], s_a1.at[0])
    whole(buf_a.at[0:63], s_a1.at[1])
    whole(st_ac.at[0:31], s_a2.at[3])
    whole(buf_cc.at[0:7], s_b1.at[3])
    whole(st_bc.at[0:7], s_b2.at[3])
    for r in range(ROUNDS):
        whole(st_a.at[r, 0:31], s_a2.at[r])
        whole(buf_c[r].at[0:7], s_b1.at[r])
        whole(st_b.at[r, 0:7], s_b2.at[r])
    whole(buf_r.at[0], s_r.at[0])
    whole(buf_r.at[1], s_r.at[1])
    whole(buf_s1.at[0:63], s_s.at[0])
    whole(buf_s2.at[0:7], s_s.at[1])


def local(coords, probes, solves, alpha, lengthscale, column_pick, plan):
    rate = math.sqrt(5.0) / lengthscale[0]
    cst = jnp.stack([
        rate * (-math.log2(math.e)), rate, rate * rate / 3.0, rate * rate / (3.0 * lengthscale[0])
    ])
    vm = pl.BlockSpec(memory_space=pltpu.VMEM)
    sm = pl.BlockSpec(memory_space=pltpu.SMEM)
    V, dma = pltpu.VMEM, pltpu.SemaphoreType.DMA
    kz, dkz, grad = pl.pallas_call(
        body,
        out_shape=[
            jax.ShapeDtypeStruct((32, COLS), F32),
            jax.ShapeDtypeStruct((32, COLS), F32),
            jax.ShapeDtypeStruct((2, 128), F32),
        ],
        in_specs=[sm, sm, sm, vm, vm, vm, vm],
        out_specs=[vm, vm, vm],
        scratch_shapes=[
            V((4, 16, 1, 128), F32),
            V((64, 8, 128), F32), V((32, 1, 128), F32),
            V((ROUNDS, 32, 2, 8, 128), F32), V((32, 4, 128), F32),
            V((ROUNDS, 8, 4, 2, 8, 128), F32), V((8, 4, 4, 128), F32),
            V((8, 4, 2, 8, 128), F32), V((8, 4, 2, 8, 128), F32), V((8, 4, 2, 8, 128), F32),
            V((8, 4, 4, 128), F32),
            V((ROUNDS, 8, 64, 128), F32), V((8, 4, 4, 128), F32),
            V((ROUNDS, 72, HALF), F32), V((8, 4, 4, 128), F32),
            V((64, COLS), F32),
            V((160, HALF), BF16), V((HALF, 8), F32),
            V((HALF, TB), BF16), V((HALF, TB), BF16), V((HALF, TB), BF16), V((HALF, TB), BF16),
            V((72, COLS), F32), V((72, COLS), F32),
            V((2, 32, COLS), F32),
            V((2, 128), F32), V((64, 2, 128), F32), V((2, 128), F32), V((8, 2, 128), F32),
            dma((2,)), dma((2,)),
            dma((4,)), dma((4,)),
            dma((4,)), dma((4,)),
            dma((4,)), dma((4,)),
            dma((2,)), dma((2,)),
            dma((2,)), dma((2,)),
        ],
        compiler_params=pltpu.CompilerParams(
            collective_id=0, has_side_effects=True, vmem_limit_bytes=40 * 2 ** 20
        ),
    )(plan, column_pick, cst, coords, alpha.reshape(1, COLS), probes, solves)
    return kz, dkz, grad[:, 0]


def solution(mesh):
    placed = (P(None, "blk"), P("pr", "blk"), P(None, "blk"), P("blk"), P(), P(), P())
    return jax.shard_map(
        local,
        mesh=mesh,
        in_specs=placed,
        out_specs=(P("pr", "blk"), P("pr", "blk"), P()),
        check_vma=False,
    )
```

```python
import math
import jax
import jax.numpy as jnp
from jax import lax
from jax.experimental import pallas as pl
from jax.experimental.pallas import tpu as pltpu
from jax.sharding import PartitionSpec as P

F32, BF16 = jnp.float32, jnp.bfloat16
MESH = pl.DeviceIdType.MESH
ROUNDS = 3
COLS = 2048
HALF = 1024
TB = 512
TA = 256
STRIP = 16
STEPS = COLS // TB


def split(value):
    hi = value.astype(BF16)
    return hi, (value - hi.astype(F32)).astype(BF16)


def tile_terms(xa, xb, ka, kb, k2):
    d2 = None
    for comp in range(3):
        off = xa[:, comp:comp + 1] - xb[comp]
        d2 = off * off if d2 is None else d2 + off * off
    dist = d2 * lax.rsqrt(jnp.maximum(d2, 1e-30))
    decay = jnp.exp2(dist * ka)
    bell = (1.0 + dist * kb) * decay
    return bell + (d2 * k2) * decay, d2 * bell


def whole(ref, sem):
    pltpu.make_async_copy(ref, ref, sem).wait()


def body(
    plan, pick, cst, coords_h, alpha_h, probes_h, solves_h,
    kz_out, dkz_out, grad_out,
    coords, alpha, probes, solves,
    comps, buf_a, buf_ac, st_a, st_ac, buf_b, buf_bc, buf_c0, buf_c1, buf_c2, buf_cc, st_b, st_bc, p32, payc,
    picked, plhs, xat, khi, klo, shi, slo, acc_k, acc_s, buf_r, sc, buf_s,
    s_in, s_a1, r_a1, s_a2, r_a2, s_b1, r_b1, s_b2, r_b2, s_r, r_r, s_s, r_s,
):
    rem, div = lax.rem, lax.div
    buf_c = (buf_c0, buf_c1, buf_c2)
    blk = lax.axis_index("blk")
    half = lax.axis_index("pr")
    core = rem(blk, 2)
    zhi = rem(div(blk, 2), 4)
    x = rem(div(blk, 8), 4)
    y = div(blk, 32)
    m_a = y * 4 + zhi
    m_b = x * 2 + core
    a64 = half * 32 + m_a
    base_a = x * 8 + core
    base_b = y * 32 + zhi * 2

    def dev_a(k):
        m = rem(k, 32)
        return {"blk": div(m, 4) * 32 + rem(m, 4) * 2 + base_a, "pr": div(k, 32)}

    def dev_b(k):
        return {"blk": base_b + div(k, 2) * 8 + rem(k, 2), "pr": half}

    def send(src, dst, ssem, rsem, dev):
        pltpu.make_async_remote_copy(
            src_ref=src, dst_ref=dst, send_sem=ssem, recv_sem=rsem, device_id=dev, device_id_type=MESH
        ).start()

    fetches = [
        pltpu.make_async_copy(src, dst, s_in.at[n])
        for n, (src, dst) in enumerate(
            [(coords_h, coords), (alpha_h, alpha), (probes_h, probes), (solves_h, solves)]
        )
    ]
    for fetch in fetches:
        fetch.start()

    shifts = [plan[r, 0] for r in range(ROUNDS)]
    t_a = [(s // 32) * 4 + (s // 2) % 4 for s in shifts]
    t_b = [((s // 8) % 4) * 2 + s % 2 for s in shifts]

    barrier = pltpu.get_barrier_semaphore()

    def greet_a(k, _):
        pl.semaphore_signal(barrier, inc=1, device_id=dev_a(rem(a64 + k, 64)), device_id_type=MESH)
        return 0

    def greet_b(k, _):
        pl.semaphore_signal(barrier, inc=1, device_id=dev_b(rem(m_b + k, 8)), device_id_type=MESH)
        return 0

    lax.fori_loop(1, 64, greet_a, 0)
    lax.fori_loop(1, 8, greet_b, 0)

    fetches[0].wait()
    fetches[1].wait()
    for g in range(4):
        row = coords[g:g + 1, :] if g < 3 else alpha[...]
        for t in range(16):
            comps[g, t] = row[:, t * 128:(t + 1) * 128]
    fetches[2].wait()
    pl.semaphore_wait(barrier, 70)

    def probe_tile(hh, yy, zz):
        rows = pl.ds(pl.multiple_of(zz * 8, 8), 8)
        return rows, pl.ds(pl.multiple_of(hh * HALF + yy * 128, 128), 128)

    def spread_comps(k, _):
        m = rem(m_a + k, 32)
        send(comps.at[rem(m, 4), half * 8 + div(m, 4)], buf_ac.at[m_a], s_a1.at[0], r_a1.at[0], dev_a(half * 32 + m))
        return 0

    def spread_probes(k, _):
        d = rem(a64 + k, 64)
        m = rem(d, 32)
        rows, cols = probe_tile(div(d, 32), div(m, 4), rem(m, 4))
        send(probes.at[rows, cols], buf_a.at[a64], s_a1.at[1], r_a1.at[1], dev_a(d))
        return 0

    lax.fori_loop(1, 32, spread_comps, 0)
    lax.fori_loop(1, 64, spread_probes, 0)
    buf_ac[m_a] = comps[zhi, half * 8 + y]
    rows, cols = probe_tile(half, y, zhi)
    buf_a[a64] = probes[rows, cols]

    whole(buf_ac.at[0:31], r_a1.at[0])

    def select_ac(k, _):
        i = rem(m_a + k, 32)
        for r in range(ROUNDS):
            st_ac[i, r:r + 1, :] = buf_ac[i ^ t_a[r]]
        st_ac[i, 3:4, :] = jnp.zeros((1, 128), F32)
        send(st_ac.at[i], buf_bc.at[y, zhi], s_a2.at[3], r_a2.at[3], dev_a(half * 32 + i))
        return 0

    lax.fori_loop(1, 32, select_ac, 0)
    for r in range(ROUNDS):
        buf_bc[y, zhi, r:r + 1, :] = buf_ac[m_a ^ t_a[r]]
    buf_bc[y, zhi, 3:4, :] = jnp.zeros((1, 128), F32)

    whole(buf_a.at[0:63], r_a1.at[1])

    def select_a(r):
        def one(k, _):
            i = rem(m_a + k, 32)
            j = i ^ t_a[r]
            st_a[r, i, 0] = buf_a[j]
            st_a[r, i, 1] = buf_a[32 + j]
            send(st_a.at[r, i], buf_b.at[r, y, zhi], s_a2.at[r], r_a2.at[r], dev_a(half * 32 + i))
            return 0

        lax.fori_loop(1, 32, one, 0)
        j = m_a ^ t_a[r]
        buf_b[r, y, zhi, 0] = buf_a[j]
        buf_b[r, y, zhi, 1] = buf_a[32 + j]

    def spread_b(r):
        whole(st_a.at[r, 0:31], r_a2.at[r])

        def one(k, _):
            d = rem(m_b + k, 8)
            send(buf_b.at[r, d], buf_c[r].at[m_b], s_b1.at[r], r_b1.at[r], dev_b(d))
            return 0

        lax.fori_loop(1, 8, one, 0)
        buf_c[r][m_b] = buf_b[r, m_b]

    def select_b(r):
        whole(buf_c[r].at[0:7], r_b1.at[r])
        cols = pl.ds(pl.multiple_of(m_b * 128, 128), 128)

        def one(k, _):
            d = rem(m_b + k, 8)
            j = d ^ t_b[r]
            for hh in range(2):
                for g in range(4):
                    lo = (hh * 4 + g) * 8
                    st_b[r, d, lo:lo + 8, :] = buf_c[r][j, g, hh]
            send(st_b.at[r, d], p32.at[r, 0:64, cols], s_b2.at[r], r_b2.at[r], dev_b(d))
            return 0

        lax.fori_loop(1, 8, one, 0)
        j = m_b ^ t_b[r]
        for hh in range(2):
            for g in range(4):
                lo = (hh * 4 + g) * 8
                p32[r, lo:lo + 8, cols] = buf_c[r][j, g, hh]

    select_a(0)

    whole(st_ac.at[0:31], r_a2.at[3])

    def spread_bc(k, _):
        d = rem(m_b + k, 8)
        send(buf_bc.at[d], buf_cc.at[m_b], s_b1.at[3], r_b1.at[3], dev_b(d))
        return 0

    lax.fori_loop(1, 8, spread_bc, 0)
    buf_cc[m_b] = buf_bc[m_b]

    spread_b(0)
    select_a(1)

    whole(buf_cc.at[0:7], r_b1.at[3])

    def select_bc(k, _):
        d = rem(m_b + k, 8)
        for r in range(ROUNDS):
            for g in range(4):
                st_bc[d, g, r:r + 1, :] = buf_cc[d ^ t_b[r], g, r:r + 1, :]
        for g in range(4):
            st_bc[d, g, 3:4, :] = jnp.zeros((1, 128), F32)
        send(st_bc.at[d], payc.at[m_b], s_b2.at[3], r_b2.at[3], dev_b(d))
        return 0

    lax.fori_loop(1, 8, select_bc, 0)
    for r in range(ROUNDS):
        for g in range(4):
            payc[m_b, g, r:r + 1, :] = buf_cc[m_b ^ t_b[r], g, r:r + 1, :]

    select_b(0)
    select_a(2)

    fetches[3].wait()
    for j in range(64):
        picked[j:j + 1, :] = solves[pl.ds(pick[j], 1), :]
    acc_k[...] = jnp.zeros_like(acc_k)
    acc_s[...] = jnp.zeros_like(acc_s)
    noise = jnp.sum(
        picked[pl.ds(pl.multiple_of(half * 32, 32), 32), :] * probes[...], axis=0, keepdims=True
    )
    own = alpha[...]
    noise = 0.5 * own * own - noise * (1.0 / 64.0)

    def fold(row):
        total = row[:, 0:128]
        for t in range(1, 16):
            total = total + row[:, t * 128:(t + 1) * 128]
        return total

    sc[0, 0:1, :] = fold(noise)

    whole(st_bc.at[0:7], r_b2.at[3])
    for r in range(ROUNDS):
        for t in range(8):
            for g in range(4):
                p32[r, 64 + g:65 + g, t * 128:(t + 1) * 128] = payc[t, g, r:r + 1, :]
        p32[r, 68:72, :] = jnp.zeros((4, HALF), F32)

    spread_b(1)

    ka, kb, k2, k_slope = cst[0], cst[1], cst[2], cst[3]
    other = pl.ds(pl.multiple_of((1 - half) * 32, 32), 32)
    mine = pl.ds(pl.multiple_of(half * 32, 32), 32)
    mate = {"blk": blk, "pr": 1 - half}

    def step(t, _):
        r = div(t, STEPS)
        chunk = rem(t, STEPS)
        b = pl.multiple_of(chunk * TB, TB)

        @pl.when(chunk == 0)
        def _prepare():
            whole(st_b.at[r, 0:7], r_b2.at[r])
            p = jnp.concatenate([p32[r], jnp.zeros((8, HALF), F32)], 0)
            hi, lo = split(p)
            plhs[0:80, :] = hi
            plhs[80:160, :] = lo
            xat[...] = jnp.transpose(p32[r, 64:72, :])

        xb = [coords[c:c + 1, pl.ds(b, TB)] for c in range(3)]
        sum_k = sum_s = None
        for a in range(0, HALF, TA):
            for st in range(a, a + TA, STRIP):
                kern, slope = tile_terms(xat[st:st + STRIP, :], xb, ka, kb, k2)
                khi[st:st + STRIP, :], klo[st:st + STRIP, :] = split(kern)
                shi[st:st + STRIP, :], slo[st:st + STRIP, :] = split(slope)
            lhs = plhs[:, a:a + TA]

            def product(hi, lo):
                one = jnp.dot(lhs, hi[a:a + TA, :], preferred_element_type=F32)
                two = jnp.dot(lhs[:80], lo[a:a + TA, :], preferred_element_type=F32)
                return one[:72] + one[80:152] + two[:72]

            more_k, more_s = product(khi, klo), product(shi, slo)
            sum_k = more_k if sum_k is None else sum_k + more_k
            sum_s = more_s if sum_s is None else sum_s + more_s
        acc_k[:, pl.ds(b, TB)] += sum_k
        acc_s[:, pl.ds(b, TB)] += sum_s

        @pl.when(t == 0)
        def _hook_0():
            select_b(1)
            spread_b(2)

        @pl.when(t == 2)
        def _hook_2():
            select_b(2)

        @pl.when(r == ROUNDS - 1)
        def _share():
            send(acc_k.at[other, pl.ds(b, TB)], buf_r.at[0, :, pl.ds(b, TB)], s_r.at[0, chunk], r_r.at[0, chunk], mate)
            send(acc_s.at[other, pl.ds(b, TB)], buf_r.at[1, :, pl.ds(b, TB)], s_r.at[1, chunk], r_r.at[1, chunk], mate)

        return 0

    lax.fori_loop(0, ROUNDS * STEPS, step, 0)

    slope = acc_s[67:68, :] * own - jnp.sum(picked[...] * acc_s[0:64, :], axis=0, keepdims=True) * (1.0 / 64.0)
    sc[0, 1:2, :] = fold(slope) * k_slope
    m_z = zhi * 2 + half

    def dev_y(k):
        return {"blk": k * 32 + rem(blk, 32), "pr": half}

    def dev_z(k):
        return {"blk": y * 32 + div(k, 2) * 2 + base_a, "pr": rem(k, 2)}

    for n, (place, device) in enumerate([(y, dev_y), (m_z, dev_z), (m_b, dev_b)]):
        def scalars(k, _):
            send(sc.at[n], buf_s.at[n, place], s_s.at[n], r_s.at[n], device(rem(place + k, 8)))
            return 0

        lax.fori_loop(1, 8, scalars, 0)
        buf_s[n, place] = sc[n]
        whole(buf_s.at[n, 0:7], r_s.at[n])
        sc[n + 1] = jnp.sum(buf_s[n], axis=0)

    total = jnp.sum(sc[3], axis=1, keepdims=True) * (0.5 / COLS)
    grad_out[...] = jnp.broadcast_to(total, (2, 128))

    for c in range(STEPS):
        cols = slice(c * TB, (c + 1) * TB)
        whole(buf_r.at[0, :, cols], r_r.at[0, c])
        kz_out[:, cols] = acc_k[mine, cols] + buf_r[0, :, cols]
        whole(buf_r.at[1, :, cols], r_r.at[1, c])
        dkz_out[:, cols] = (acc_s[mine, cols] + buf_r[1, :, cols]) * k_slope

    whole(buf_ac.at[0:31], s_a1.at[0])
    whole(buf_a.at[0:63], s_a1.at[1])
    whole(st_ac.at[0:31], s_a2.at[3])
    whole(buf_cc.at[0:7], s_b1.at[3])
    whole(st_bc.at[0:7], s_b2.at[3])
    for r in range(ROUNDS):
        whole(st_a.at[r, 0:31], s_a2.at[r])
        whole(buf_c[r].at[0:7], s_b1.at[r])
        whole(st_b.at[r, 0:7], s_b2.at[r])
        whole(buf_s.at[r, 0:7], s_s.at[r])
    for c in range(STEPS):
        cols = slice(c * TB, (c + 1) * TB)
        whole(buf_r.at[0, :, cols], s_r.at[0, c])
        whole(buf_r.at[1, :, cols], s_r.at[1, c])


def local(coords, probes, solves, alpha, lengthscale, column_pick, plan):
    rate = math.sqrt(5.0) / lengthscale[0]
    cst = jnp.stack([
        rate * (-math.log2(math.e)), rate, rate * rate / 3.0, rate * rate / (3.0 * lengthscale[0])
    ])
    vm = pl.BlockSpec(memory_space=pltpu.VMEM)
    sm = pl.BlockSpec(memory_space=pltpu.SMEM)
    hb = pl.BlockSpec(memory_space=pl.ANY)
    V, dma = pltpu.VMEM, pltpu.SemaphoreType.DMA
    kz, dkz, grad = pl.pallas_call(
        body,
        out_shape=[
            jax.ShapeDtypeStruct((32, COLS), F32),
            jax.ShapeDtypeStruct((32, COLS), F32),
            jax.ShapeDtypeStruct((2, 128), F32),
        ],
        in_specs=[sm, sm, sm, hb, hb, hb, hb],
        out_specs=[vm, vm, vm],
        scratch_shapes=[
            V((3, COLS), F32), V((1, COLS), F32), V((32, COLS), F32), V((64, COLS), F32),
            V((4, 16, 1, 128), F32),
            V((64, 8, 128), F32), V((32, 1, 128), F32),
            V((ROUNDS, 32, 2, 8, 128), F32), V((32, 4, 128), F32),
            V((ROUNDS, 8, 4, 2, 8, 128), F32), V((8, 4, 4, 128), F32),
            V((8, 4, 2, 8, 128), F32), V((8, 4, 2, 8, 128), F32), V((8, 4, 2, 8, 128), F32),
            V((8, 4, 4, 128), F32),
            V((ROUNDS, 8, 64, 128), F32), V((8, 4, 4, 128), F32),
            V((ROUNDS, 72, HALF), F32), V((8, 4, 4, 128), F32),
            V((64, COLS), F32),
            V((160, HALF), BF16), V((HALF, 8), F32),
            V((HALF, TB), BF16), V((HALF, TB), BF16), V((HALF, TB), BF16), V((HALF, TB), BF16),
            V((72, COLS), F32), V((72, COLS), F32),
            V((2, 32, COLS), F32),
            V((4, 2, 128), F32), V((3, 8, 2, 128), F32),
            dma((4,)),
            dma((2,)), dma((2,)),
            dma((4,)), dma((4,)),
            dma((4,)), dma((4,)),
            dma((4,)), dma((4,)),
            dma((2, STEPS)), dma((2, STEPS)),
            dma((3,)), dma((3,)),
        ],
        compiler_params=pltpu.CompilerParams(
            collective_id=0, has_side_effects=True, vmem_limit_bytes=40 * 2 ** 20
        ),
    )(plan, column_pick, cst, coords, alpha.reshape(1, COLS), probes, solves)
    return kz, dkz, grad[:, 0]


def solution(mesh):
    placed = (P(None, "blk"), P("pr", "blk"), P(None, "blk"), P("blk"), P(), P(), P())
    return jax.shard_map(
        local,
        mesh=mesh,
        in_specs=placed,
        out_specs=(P("pr", "blk"), P("pr", "blk"), P()),
        check_vma=False,
    )
```

```python
import math
import jax
import jax.numpy as jnp
from jax import lax
from jax.experimental import pallas as pl
from jax.experimental.pallas import tpu as pltpu
from jax.sharding import PartitionSpec as P

F32, BF16 = jnp.float32, jnp.bfloat16
MESH = pl.DeviceIdType.MESH
ROUNDS = 3
COLS = 2048
HALF = 1024
TB = 256
LAG = 11
RING = 6
STRIP = 16
STEPS = COLS // TB


def split(value):
    hi = value.astype(BF16)
    return hi, (value - hi.astype(F32)).astype(BF16)


def tile_terms(xa, xb, ka, kb, k2):
    d2 = None
    for comp in range(3):
        off = xa[:, comp:comp + 1] - xb[comp]
        d2 = off * off if d2 is None else d2 + off * off
    dist = d2 * lax.rsqrt(jnp.maximum(d2, 1e-30))
    decay = jnp.exp2(dist * ka)
    bell = (1.0 + dist * kb) * decay
    return bell + (d2 * k2) * decay, d2 * bell


def whole(ref, sem):
    pltpu.make_async_copy(ref, ref, sem).wait()


def body(
    plan, pick, cst, coords_h, alpha_h, probes_h, solves_h,
    kz_out, dkz_out, grad_out,
    coords, alpha, probes, solves,
    comps, buf_a, buf_ac, st_a, st_ac, buf_b, buf_bc, buf_c0, buf_c1, buf_c2, buf_cc, st_b, st_bc, p32, payc,
    picked, plhs, xat, even, odd, acc_k, acc_s, buf_r, sc, buf_s, buf_s2,
    s_in, s_a1, r_a1, s_a2, r_a2, s_b1, r_b1, s_b2, r_b2, s_r, r_r, s_rs, r_rs, s_s, r_s,
):
    rem, div = lax.rem, lax.div
    buf_c = (buf_c0, buf_c1, buf_c2)
    blk = lax.axis_index("blk")
    half = lax.axis_index("pr")
    core = rem(blk, 2)
    zhi = rem(div(blk, 2), 4)
    x = rem(div(blk, 8), 4)
    y = div(blk, 32)
    m_a = y * 4 + zhi
    m_b = x * 2 + core
    a64 = half * 32 + m_a
    base_a = x * 8 + core
    base_b = y * 32 + zhi * 2

    def dev_a(k):
        m = rem(k, 32)
        return {"blk": div(m, 4) * 32 + rem(m, 4) * 2 + base_a, "pr": div(k, 32)}

    def dev_b(k):
        return {"blk": base_b + div(k, 2) * 8 + rem(k, 2), "pr": half}

    def send(src, dst, ssem, rsem, dev):
        pltpu.make_async_remote_copy(
            src_ref=src, dst_ref=dst, send_sem=ssem, recv_sem=rsem, device_id=dev, device_id_type=MESH
        ).start()

    fetches = [
        pltpu.make_async_copy(src, dst, s_in.at[n])
        for n, (src, dst) in enumerate(
            [(coords_h, coords), (alpha_h, alpha), (probes_h, probes), (solves_h, solves)]
        )
    ]
    for fetch in fetches:
        fetch.start()

    shifts = [plan[r, 0] for r in range(ROUNDS)]
    t_a = [(s // 32) * 4 + (s // 2) % 4 for s in shifts]
    t_b = [((s // 8) % 4) * 2 + s % 2 for s in shifts]

    barrier = pltpu.get_barrier_semaphore()

    def greet_a(k, _):
        pl.semaphore_signal(barrier, inc=1, device_id=dev_a(rem(a64 + k, 64)), device_id_type=MESH)
        return 0

    def greet_b(k, _):
        pl.semaphore_signal(barrier, inc=1, device_id=dev_b(rem(m_b + k, 8)), device_id_type=MESH)
        return 0

    lax.fori_loop(1, 64, greet_a, 0)
    lax.fori_loop(1, 8, greet_b, 0)

    fetches[0].wait()
    fetches[1].wait()
    for g in range(4):
        row = coords[g:g + 1, :] if g < 3 else alpha[...]
        for t in range(16):
            comps[g, t] = row[:, t * 128:(t + 1) * 128]
    fetches[2].wait()
    pl.semaphore_wait(barrier, 70)

    def probe_tile(hh, yy, zz):
        rows = pl.ds(pl.multiple_of(zz * 8, 8), 8)
        return rows, pl.ds(pl.multiple_of(hh * HALF + yy * 128, 128), 128)

    def spread_comps(k, _):
        m = rem(m_a + k, 32)
        send(comps.at[rem(m, 4), half * 8 + div(m, 4)], buf_ac.at[m_a], s_a1.at[0], r_a1.at[0], dev_a(half * 32 + m))
        return 0

    def spread_probes(k, _):
        d = rem(a64 + k, 64)
        m = rem(d, 32)
        rows, cols = probe_tile(div(d, 32), div(m, 4), rem(m, 4))
        send(probes.at[rows, cols], buf_a.at[a64], s_a1.at[1], r_a1.at[1], dev_a(d))
        return 0

    lax.fori_loop(1, 32, spread_comps, 0)
    lax.fori_loop(1, 64, spread_probes, 0)
    buf_ac[m_a] = comps[zhi, half * 8 + y]
    rows, cols = probe_tile(half, y, zhi)
    buf_a[a64] = probes[rows, cols]

    whole(buf_ac.at[0:31], r_a1.at[0])

    def select_ac(k, _):
        i = rem(m_a + k, 32)
        for r in range(ROUNDS):
            st_ac[i, r:r + 1, :] = buf_ac[i ^ t_a[r]]
        st_ac[i, 3:4, :] = jnp.zeros((1, 128), F32)
        send(st_ac.at[i], buf_bc.at[y, zhi], s_a2.at[3], r_a2.at[3], dev_a(half * 32 + i))
        return 0

    lax.fori_loop(1, 32, select_ac, 0)
    for r in range(ROUNDS):
        buf_bc[y, zhi, r:r + 1, :] = buf_ac[m_a ^ t_a[r]]
    buf_bc[y, zhi, 3:4, :] = jnp.zeros((1, 128), F32)

    def select_a(r):
        def one(k, _):
            i = rem(m_a + k, 32)
            j = i ^ t_a[r]
            st_a[r, i, 0] = buf_a[j]
            st_a[r, i, 1] = buf_a[32 + j]
            send(st_a.at[r, i], buf_b.at[r, y, zhi], s_a2.at[r], r_a2.at[r], dev_a(half * 32 + i))
            return 0

        lax.fori_loop(1, 32, one, 0)
        j = m_a ^ t_a[r]
        buf_b[r, y, zhi, 0] = buf_a[j]
        buf_b[r, y, zhi, 1] = buf_a[32 + j]

    def spread_b(r):
        whole(st_a.at[r, 0:31], r_a2.at[r])

        def one(k, _):
            d = rem(m_b + k, 8)
            send(buf_b.at[r, d], buf_c[r].at[m_b], s_b1.at[r], r_b1.at[r], dev_b(d))
            return 0

        lax.fori_loop(1, 8, one, 0)
        buf_c[r][m_b] = buf_b[r, m_b]

    def select_b(r):
        whole(buf_c[r].at[0:7], r_b1.at[r])
        cols = pl.ds(pl.multiple_of(m_b * 128, 128), 128)

        def one(k, _):
            d = rem(m_b + k, 8)
            j = d ^ t_b[r]
            for hh in range(2):
                for g in range(4):
                    lo = (hh * 4 + g) * 8
                    st_b[r, d, lo:lo + 8, :] = buf_c[r][j, g, hh]
            send(st_b.at[r, d], p32.at[r, 0:64, cols], s_b2.at[r], r_b2.at[r], dev_b(d))
            return 0

        lax.fori_loop(1, 8, one, 0)
        j = m_b ^ t_b[r]
        for hh in range(2):
            for g in range(4):
                lo = (hh * 4 + g) * 8
                p32[r, lo:lo + 8, cols] = buf_c[r][j, g, hh]

    whole(buf_a.at[0:63], r_a1.at[1])
    for r in range(ROUNDS):
        select_a(r)
    whole(st_ac.at[0:31], r_a2.at[3])

    def spread_bc(k, _):
        d = rem(m_b + k, 8)
        send(buf_bc.at[d], buf_cc.at[m_b], s_b1.at[3], r_b1.at[3], dev_b(d))
        return 0

    lax.fori_loop(1, 8, spread_bc, 0)
    buf_cc[m_b] = buf_bc[m_b]
    whole(buf_cc.at[0:7], r_b1.at[3])

    def select_bc(k, _):
        d = rem(m_b + k, 8)
        for r in range(ROUNDS):
            for g in range(4):
                st_bc[d, g, r:r + 1, :] = buf_cc[d ^ t_b[r], g, r:r + 1, :]
        for g in range(4):
            st_bc[d, g, 3:4, :] = jnp.zeros((1, 128), F32)
        send(st_bc.at[d], payc.at[m_b], s_b2.at[3], r_b2.at[3], dev_b(d))
        return 0

    lax.fori_loop(1, 8, select_bc, 0)
    for r in range(ROUNDS):
        for g in range(4):
            payc[m_b, g, r:r + 1, :] = buf_cc[m_b ^ t_b[r], g, r:r + 1, :]

    whole(st_bc.at[0:7], r_b2.at[3])
    for r in range(ROUNDS):
        for t in range(8):
            for g in range(4):
                p32[r, 64 + g:65 + g, t * 128:(t + 1) * 128] = payc[t, g, r:r + 1, :]
        p32[r, 68:72, :] = jnp.zeros((4, HALF), F32)
        xat[r] = jnp.transpose(p32[r, 64:72, :])

    ka, kb, k2, k_slope = cst[0], cst[1], cst[2], cst[3]
    other = pl.ds(pl.multiple_of((1 - half) * 32, 32), 32)
    mine = pl.ds(pl.multiple_of(half * 32, 32), 32)
    mate = {"blk": blk, "pr": 1 - half}

    def columns(t):
        return pl.ds(pl.multiple_of(rem(t, STEPS) * TB, TB), TB)

    def tiles(t, ring):
        r, slot = div(t, STEPS), rem(div(t, 2), RING)
        xb = [coords[c:c + 1, columns(t)] for c in range(3)]
        for st in range(0, HALF, STRIP):
            kern, slope = tile_terms(xat[r, st:st + STRIP, :], xb, ka, kb, k2)
            ring[slot, 0, st:st + STRIP, :], ring[slot, 1, st:st + STRIP, :] = split(kern)
            ring[slot, 2, st:st + STRIP, :], ring[slot, 3, st:st + STRIP, :] = split(slope)

    def product(n, acc, t, ring):
        r, slot = div(t, STEPS), rem(div(t, 2), RING)
        one = jnp.dot(plhs[r], ring[slot, 2 * n], preferred_element_type=F32)
        two = jnp.dot(plhs[r, 0:80, :], ring[slot, 2 * n + 1], preferred_element_type=F32)
        acc[:, columns(t)] += one[:72] + one[80:152] + two[:72]

    def products(t, ring):
        product(0, acc_k, t, ring)
        product(1, acc_s, t, ring)

    def prepare(r):
        whole(st_b.at[r, 0:7], r_b2.at[r])
        hi, lo = split(jnp.concatenate([p32[r], jnp.zeros((8, HALF), F32)], 0))
        plhs[r, 0:80, :] = hi
        plhs[r, 80:160, :] = lo

    def first(i, _):
        tiles(2 * i, even)
        tiles(2 * i + 1, odd)

        @pl.when(i == 1)
        def _hook_1():
            spread_b(0)

        @pl.when(i == 3)
        def _hook_3():
            select_b(0)

        @pl.when(i == 4)
        def _hook_4():
            spread_b(1)

        return 0

    lax.fori_loop(0, LAG // 2, first, 0)
    tiles(LAG - 1, even)

    fetches[3].wait()
    for j in range(64):
        picked[j:j + 1, :] = solves[pl.ds(pick[j], 1), :]
    acc_k[...] = jnp.zeros_like(acc_k)
    acc_s[...] = jnp.zeros_like(acc_s)
    noise = jnp.sum(picked[mine, :] * probes[...], axis=0, keepdims=True)
    own = alpha[...]
    noise = 0.5 * own * own - noise * (1.0 / 64.0)

    def fold(row):
        total = row[:, 0:128]
        for t in range(1, 16):
            total = total + row[:, t * 128:(t + 1) * 128]
        return total

    sc[0, 0:1, :] = fold(noise)
    prepare(0)

    def second(i, _):
        tiles(2 * i + LAG, odd)
        products(2 * i, even)
        tiles(2 * i + LAG + 1, even)
        products(2 * i + 1, odd)

        @pl.when(i == 0)
        def _hook_0():
            select_b(1)
            spread_b(2)

        @pl.when(i == 2)
        def _hook_2():
            select_b(2)

        @pl.when(i == 3)
        def _hook_3():
            prepare(1)

        return 0

    total_steps = ROUNDS * STEPS
    pairs = (total_steps - LAG) // 2
    lax.fori_loop(0, pairs, second, 0)
    tiles(total_steps - 1, odd)
    products(2 * pairs, even)
    prepare(2)

    def last_slope(i, _):
        t = 2 * pairs + 1 + 2 * i
        product(1, acc_s, t, odd)
        product(1, acc_s, t + 1, even)
        return 0

    lax.fori_loop(0, LAG // 2, last_slope, 0)
    product(1, acc_s, total_steps - 1, odd)

    slope = acc_s[67:68, :] * own - jnp.sum(picked[...] * acc_s[0:64, :], axis=0, keepdims=True) * (1.0 / 64.0)
    sc[0, 1:2, :] = fold(slope) * k_slope

    def scalars_a(k, _):
        send(sc.at[0], buf_s.at[a64], s_s.at[0], r_s.at[0], dev_a(rem(a64 + k, 64)))
        return 0

    lax.fori_loop(1, 64, scalars_a, 0)
    buf_s[a64] = sc[0]

    for c in range(2):
        cols = slice(c * HALF, (c + 1) * HALF)
        send(acc_s.at[other, cols], buf_r.at[1, :, cols], s_rs.at[c], r_rs.at[c], mate)

    def share(t):
        @pl.when(t >= total_steps - STEPS)
        def _share():
            chunk, cols = rem(t, STEPS), columns(t)
            send(acc_k.at[other, cols], buf_r.at[0, :, cols], s_r.at[chunk], r_r.at[chunk], mate)

    def last_kernel(i, _):
        t = 2 * pairs + 1 + 2 * i
        product(0, acc_k, t, odd)
        share(t)
        product(0, acc_k, t + 1, even)
        share(t + 1)
        return 0

    lax.fori_loop(0, LAG // 2, last_kernel, 0)
    product(0, acc_k, total_steps - 1, odd)
    share(jnp.int32(total_steps - 1))

    whole(buf_s.at[0:63], r_s.at[0])
    sc[1] = jnp.sum(buf_s[...], axis=0)

    def scalars_b(k, _):
        send(sc.at[1], buf_s2.at[m_b], s_s.at[1], r_s.at[1], dev_b(rem(m_b + k, 8)))
        return 0

    lax.fori_loop(1, 8, scalars_b, 0)
    buf_s2[m_b] = sc[1]

    for c in range(2):
        cols = slice(c * HALF, (c + 1) * HALF)
        whole(buf_r.at[1, :, cols], r_rs.at[c])
        dkz_out[:, cols] = (acc_s[mine, cols] + buf_r[1, :, cols]) * k_slope
    for c in range(STEPS):
        cols = slice(c * TB, (c + 1) * TB)
        whole(buf_r.at[0, :, cols], r_r.at[c])
        kz_out[:, cols] = acc_k[mine, cols] + buf_r[0, :, cols]

    whole(buf_s2.at[0:7], r_s.at[1])
    total = jnp.sum(jnp.sum(buf_s2[...], axis=0), axis=1, keepdims=True) * (0.5 / COLS)
    grad_out[...] = jnp.broadcast_to(total, (2, 128))

    whole(buf_ac.at[0:31], s_a1.at[0])
    whole(buf_a.at[0:63], s_a1.at[1])
    whole(st_ac.at[0:31], s_a2.at[3])
    whole(buf_cc.at[0:7], s_b1.at[3])
    whole(st_bc.at[0:7], s_b2.at[3])
    for r in range(ROUNDS):
        whole(st_a.at[r, 0:31], s_a2.at[r])
        whole(buf_c[r].at[0:7], s_b1.at[r])
        whole(st_b.at[r, 0:7], s_b2.at[r])
    whole(buf_s.at[0:63], s_s.at[0])
    whole(buf_s2.at[0:7], s_s.at[1])
    for c in range(2):
        whole(buf_r.at[1, :, c * HALF:(c + 1) * HALF], s_rs.at[c])
    for c in range(STEPS):
        whole(buf_r.at[0, :, c * TB:(c + 1) * TB], s_r.at[c])


def local(coords, probes, solves, alpha, lengthscale, column_pick, plan):
    rate = math.sqrt(5.0) / lengthscale[0]
    cst = jnp.stack([
        rate * (-math.log2(math.e)), rate, rate * rate / 3.0, rate * rate / (3.0 * lengthscale[0])
    ])
    vm = pl.BlockSpec(memory_space=pltpu.VMEM)
    sm = pl.BlockSpec(memory_space=pltpu.SMEM)
    hb = pl.BlockSpec(memory_space=pl.ANY)
    V, dma = pltpu.VMEM, pltpu.SemaphoreType.DMA
    kz, dkz, grad = pl.pallas_call(
        body,
        out_shape=[
            jax.ShapeDtypeStruct((32, COLS), F32),
            jax.ShapeDtypeStruct((32, COLS), F32),
            jax.ShapeDtypeStruct((2, 128), F32),
        ],
        in_specs=[sm, sm, sm, hb, hb, hb, hb],
        out_specs=[vm, vm, vm],
        scratch_shapes=[
            V((3, COLS), F32), V((1, COLS), F32), V((32, COLS), F32), V((64, COLS), F32),
            V((4, 16, 1, 128), F32),
            V((64, 8, 128), F32), V((32, 1, 128), F32),
            V((ROUNDS, 32, 2, 8, 128), F32), V((32, 4, 128), F32),
            V((ROUNDS, 8, 4, 2, 8, 128), F32), V((8, 4, 4, 128), F32),
            V((8, 4, 2, 8, 128), F32), V((8, 4, 2, 8, 128), F32), V((8, 4, 2, 8, 128), F32),
            V((8, 4, 4, 128), F32),
            V((ROUNDS, 8, 64, 128), F32), V((8, 4, 4, 128), F32),
            V((ROUNDS, 72, HALF), F32), V((8, 4, 4, 128), F32),
            V((64, COLS), F32),
            V((ROUNDS, 160, HALF), BF16), V((ROUNDS, HALF, 8), F32),
            V((RING, 4, HALF, TB), BF16), V((RING, 4, HALF, TB), BF16),
            V((72, COLS), F32), V((72, COLS), F32),
            V((2, 32, COLS), F32),
            V((2, 2, 128), F32), V((64, 2, 128), F32), V((8, 2, 128), F32),
            dma((4,)),
            dma((2,)), dma((2,)),
            dma((4,)), dma((4,)),
            dma((4,)), dma((4,)),
            dma((4,)), dma((4,)),
            dma((STEPS,)), dma((STEPS,)),
            dma((2,)), dma((2,)),
            dma((2,)), dma((2,)),
        ],
        compiler_params=pltpu.CompilerParams(
            collective_id=0, has_side_effects=True, vmem_limit_bytes=63 * 2 ** 20
        ),
    )(plan, column_pick, cst, coords, alpha.reshape(1, COLS), probes, solves)
    return kz, dkz, grad[:, 0]


def solution(mesh):
    placed = (P(None, "blk"), P("pr", "blk"), P(None, "blk"), P("blk"), P(), P(), P())
    return jax.shard_map(
        local,
        mesh=mesh,
        in_specs=placed,
        out_specs=(P("pr", "blk"), P("pr", "blk"), P()),
        check_vma=False,
    )
```

```python
import math
import jax
import jax.numpy as jnp
from jax import lax
from jax.experimental import pallas as pl
from jax.experimental.pallas import tpu as pltpu
from jax.sharding import PartitionSpec as P

F32, BF16 = jnp.float32, jnp.bfloat16
MESH = pl.DeviceIdType.MESH
ROUNDS = 3
COLS = 2048
HALF = 1024
TB = 256
LAG = 15
RING = 8
STRIP = 16
STEPS = COLS // TB


def split(value):
    hi = value.astype(BF16)
    return hi, (value - hi.astype(F32)).astype(BF16)


def tile_terms(xa, xb, ka, kb, k2):
    d2 = None
    for comp in range(3):
        off = xa[:, comp:comp + 1] - xb[comp]
        d2 = off * off if d2 is None else d2 + off * off
    dist = d2 * lax.rsqrt(jnp.maximum(d2, 1e-30))
    decay = jnp.exp2(dist * ka)
    bell = (1.0 + dist * kb) * decay
    return bell + (d2 * k2) * decay, d2 * bell


def whole(ref, sem):
    pltpu.make_async_copy(ref, ref, sem).wait()


def body(
    plan, pick, cst, coords_h, alpha_h, probes_h, solves_h,
    kz_out, dkz_out, grad_out,
    coords, alpha, probes, solves,
    comps, buf_a, buf_ac, st_a, st_ac, buf_b, buf_bc, buf_c0, buf_c1, buf_c2, buf_cc, st_b, st_bc, p32, payc,
    picked, plhs, xat, even, odd, acc_k, acc_s, buf_r, sc, buf_s, buf_s2,
    s_in, s_a1, r_a1, s_a2, r_a2, s_b1, r_b1, s_b2, r_b2, s_r, r_r, s_rs, r_rs, s_s, r_s,
):
    rem, div = lax.rem, lax.div
    buf_c = (buf_c0, buf_c1, buf_c2)
    blk = lax.axis_index("blk")
    half = lax.axis_index("pr")
    core = rem(blk, 2)
    zhi = rem(div(blk, 2), 4)
    x = rem(div(blk, 8), 4)
    y = div(blk, 32)
    m_a = y * 4 + zhi
    m_b = x * 2 + core
    a64 = half * 32 + m_a
    base_a = x * 8 + core
    base_b = y * 32 + zhi * 2

    def dev_a(k):
        m = rem(k, 32)
        return {"blk": div(m, 4) * 32 + rem(m, 4) * 2 + base_a, "pr": div(k, 32)}

    def dev_b(k):
        return {"blk": base_b + div(k, 2) * 8 + rem(k, 2), "pr": half}

    def send(src, dst, ssem, rsem, dev):
        pltpu.make_async_remote_copy(
            src_ref=src, dst_ref=dst, send_sem=ssem, recv_sem=rsem, device_id=dev, device_id_type=MESH
        ).start()

    fetches = [
        pltpu.make_async_copy(src, dst, s_in.at[n])
        for n, (src, dst) in enumerate(
            [(coords_h, coords), (alpha_h, alpha), (probes_h, probes), (solves_h, solves)]
        )
    ]
    for fetch in fetches:
        fetch.start()

    shifts = [plan[r, 0] for r in range(ROUNDS)]
    t_a = [(s // 32) * 4 + (s // 2) % 4 for s in shifts]
    t_b = [((s // 8) % 4) * 2 + s % 2 for s in shifts]

    barrier = pltpu.get_barrier_semaphore()

    def greet_a(k, _):
        pl.semaphore_signal(barrier, inc=1, device_id=dev_a(rem(a64 + k, 64)), device_id_type=MESH)
        return 0

    def greet_b(k, _):
        pl.semaphore_signal(barrier, inc=1, device_id=dev_b(rem(m_b + k, 8)), device_id_type=MESH)
        return 0

    lax.fori_loop(1, 64, greet_a, 0)
    lax.fori_loop(1, 8, greet_b, 0)

    fetches[0].wait()
    fetches[1].wait()
    for g in range(4):
        row = coords[g:g + 1, :] if g < 3 else alpha[...]
        for t in range(16):
            comps[g, t] = row[:, t * 128:(t + 1) * 128]
    fetches[2].wait()
    pl.semaphore_wait(barrier, 70)

    def probe_tile(hh, yy, zz):
        rows = pl.ds(pl.multiple_of(zz * 8, 8), 8)
        return rows, pl.ds(pl.multiple_of(hh * HALF + yy * 128, 128), 128)

    def spread_comps(k, _):
        m = rem(m_a + k, 32)
        send(comps.at[rem(m, 4), half * 8 + div(m, 4)], buf_ac.at[m_a], s_a1.at[0], r_a1.at[0], dev_a(half * 32 + m))
        return 0

    def spread_probes(k, _):
        d = rem(a64 + k, 64)
        m = rem(d, 32)
        rows, cols = probe_tile(div(d, 32), div(m, 4), rem(m, 4))
        send(probes.at[rows, cols], buf_a.at[a64], s_a1.at[1], r_a1.at[1], dev_a(d))
        return 0

    lax.fori_loop(1, 32, spread_comps, 0)
    lax.fori_loop(1, 64, spread_probes, 0)
    buf_ac[m_a] = comps[zhi, half * 8 + y]
    rows, cols = probe_tile(half, y, zhi)
    buf_a[a64] = probes[rows, cols]

    other = pl.ds(pl.multiple_of((1 - half) * 32, 32), 32)
    mine = pl.ds(pl.multiple_of(half * 32, 32), 32)
    mate = {"blk": blk, "pr": 1 - half}

    fetches[3].wait()
    for j in range(64):
        picked[j:j + 1, :] = solves[pl.ds(pick[j], 1), :]
    acc_k[...] = jnp.zeros_like(acc_k)
    acc_s[...] = jnp.zeros_like(acc_s)
    noise = jnp.sum(picked[mine, :] * probes[...], axis=0, keepdims=True)
    own = alpha[...]
    noise = 0.5 * own * own - noise * (1.0 / 64.0)

    def fold(row):
        total = row[:, 0:128]
        for t in range(1, 16):
            total = total + row[:, t * 128:(t + 1) * 128]
        return total

    sc[0, 0:1, :] = fold(noise)
    whole(buf_ac.at[0:31], r_a1.at[0])

    def select_ac(k, _):
        i = rem(m_a + k, 32)
        for r in range(ROUNDS):
            st_ac[i, r:r + 1, :] = buf_ac[i ^ t_a[r]]
        st_ac[i, 3:4, :] = jnp.zeros((1, 128), F32)
        send(st_ac.at[i], buf_bc.at[y, zhi], s_a2.at[3], r_a2.at[3], dev_a(half * 32 + i))
        return 0

    lax.fori_loop(1, 32, select_ac, 0)
    for r in range(ROUNDS):
        buf_bc[y, zhi, r:r + 1, :] = buf_ac[m_a ^ t_a[r]]
    buf_bc[y, zhi, 3:4, :] = jnp.zeros((1, 128), F32)

    def select_a(r):
        def one(k, _):
            i = rem(m_a + k, 32)
            j = i ^ t_a[r]
            st_a[r, i, 0] = buf_a[j]
            st_a[r, i, 1] = buf_a[32 + j]
            send(st_a.at[r, i], buf_b.at[r, y, zhi], s_a2.at[r], r_a2.at[r], dev_a(half * 32 + i))
            return 0

        lax.fori_loop(1, 32, one, 0)
        j = m_a ^ t_a[r]
        buf_b[r, y, zhi, 0] = buf_a[j]
        buf_b[r, y, zhi, 1] = buf_a[32 + j]

    def spread_b(r):
        whole(st_a.at[r, 0:31], r_a2.at[r])

        def one(k, _):
            d = rem(m_b + k, 8)
            send(buf_b.at[r, d], buf_c[r].at[m_b], s_b1.at[r], r_b1.at[r], dev_b(d))
            return 0

        lax.fori_loop(1, 8, one, 0)
        buf_c[r][m_b] = buf_b[r, m_b]

    def select_b(r):
        whole(buf_c[r].at[0:7], r_b1.at[r])
        cols = pl.ds(pl.multiple_of(m_b * 128, 128), 128)

        def one(k, _):
            d = rem(m_b + k, 8)
            j = d ^ t_b[r]
            for hh in range(2):
                for g in range(4):
                    lo = (hh * 4 + g) * 8
                    st_b[r, d, lo:lo + 8, :] = buf_c[r][j, g, hh]
            send(st_b.at[r, d], p32.at[r, 0:64, cols], s_b2.at[r], r_b2.at[r], dev_b(d))
            return 0

        lax.fori_loop(1, 8, one, 0)
        j = m_b ^ t_b[r]
        for hh in range(2):
            for g in range(4):
                lo = (hh * 4 + g) * 8
                p32[r, lo:lo + 8, cols] = buf_c[r][j, g, hh]

    whole(buf_a.at[0:63], r_a1.at[1])
    for r in range(ROUNDS):
        select_a(r)
    whole(st_ac.at[0:31], r_a2.at[3])

    def spread_bc(k, _):
        d = rem(m_b + k, 8)
        send(buf_bc.at[d], buf_cc.at[m_b], s_b1.at[3], r_b1.at[3], dev_b(d))
        return 0

    lax.fori_loop(1, 8, spread_bc, 0)
    buf_cc[m_b] = buf_bc[m_b]
    whole(buf_cc.at[0:7], r_b1.at[3])

    def select_bc(k, _):
        d = rem(m_b + k, 8)
        for r in range(ROUNDS):
            for g in range(4):
                st_bc[d, g, r:r + 1, :] = buf_cc[d ^ t_b[r], g, r:r + 1, :]
        for g in range(4):
            st_bc[d, g, 3:4, :] = jnp.zeros((1, 128), F32)
        send(st_bc.at[d], payc.at[m_b], s_b2.at[3], r_b2.at[3], dev_b(d))
        return 0

    lax.fori_loop(1, 8, select_bc, 0)
    for r in range(ROUNDS):
        for g in range(4):
            payc[m_b, g, r:r + 1, :] = buf_cc[m_b ^ t_b[r], g, r:r + 1, :]

    whole(st_bc.at[0:7], r_b2.at[3])
    for r in range(ROUNDS):
        for t in range(8):
            for g in range(4):
                p32[r, 64 + g:65 + g, t * 128:(t + 1) * 128] = payc[t, g, r:r + 1, :]
        p32[r, 68:72, :] = jnp.zeros((4, HALF), F32)
        xat[r] = jnp.transpose(p32[r, 64:72, :])

    ka, kb, k2, k_slope = cst[0], cst[1], cst[2], cst[3]

    def columns(t):
        return pl.ds(pl.multiple_of(rem(t, STEPS) * TB, TB), TB)

    def tiles(t, ring):
        r, slot = div(t, STEPS), rem(div(t, 2), RING)
        xb = [coords[c:c + 1, columns(t)] for c in range(3)]
        for st in range(0, HALF, STRIP):
            kern, slope = tile_terms(xat[r, st:st + STRIP, :], xb, ka, kb, k2)
            ring[slot, 0, st:st + STRIP, :], ring[slot, 1, st:st + STRIP, :] = split(kern)
            ring[slot, 2, st:st + STRIP, :], ring[slot, 3, st:st + STRIP, :] = split(slope)

    def product(n, acc, t, ring):
        r, slot = div(t, STEPS), rem(div(t, 2), RING)
        one = jnp.dot(plhs[r], ring[slot, 2 * n], preferred_element_type=F32)
        two = jnp.dot(plhs[r, 0:80, :], ring[slot, 2 * n + 1], preferred_element_type=F32)
        acc[:, columns(t)] += one[:72] + one[80:152] + two[:72]

    def products(t, ring):
        product(0, acc_k, t, ring)
        product(1, acc_s, t, ring)

    def prepare(r):
        whole(st_b.at[r, 0:7], r_b2.at[r])
        hi, lo = split(jnp.concatenate([p32[r], jnp.zeros((8, HALF), F32)], 0))
        plhs[r, 0:80, :] = hi
        plhs[r, 80:160, :] = lo

    def first(i, _):
        tiles(2 * i, even)
        tiles(2 * i + 1, odd)

        @pl.when(i == 0)
        def _hook_0():
            spread_b(0)

        @pl.when(i == 2)
        def _hook_2():
            spread_b(1)
            select_b(0)

        @pl.when(i == 4)
        def _hook_4():
            spread_b(2)
            select_b(1)

        @pl.when(i == 6)
        def _hook_6():
            select_b(2)

        return 0

    lax.fori_loop(0, LAG // 2, first, 0)
    tiles(LAG - 1, even)

    prepare(0)

    def second(i, _):
        tiles(2 * i + LAG, odd)
        products(2 * i, even)
        tiles(2 * i + LAG + 1, even)
        products(2 * i + 1, odd)

        return 0

    total_steps = ROUNDS * STEPS
    pairs = (total_steps - LAG) // 2
    lax.fori_loop(0, pairs, second, 0)
    prepare(1)
    tiles(total_steps - 1, odd)
    products(2 * pairs, even)
    prepare(2)

    def last_slope(i, _):
        t = 2 * pairs + 1 + 2 * i
        product(1, acc_s, t, odd)
        product(1, acc_s, t + 1, even)
        return 0

    lax.fori_loop(0, LAG // 2, last_slope, 0)
    product(1, acc_s, total_steps - 1, odd)

    slope = acc_s[67:68, :] * own - jnp.sum(picked[...] * acc_s[0:64, :], axis=0, keepdims=True) * (1.0 / 64.0)
    sc[0, 1:2, :] = fold(slope) * k_slope

    def scalars_a(k, _):
        send(sc.at[0], buf_s.at[a64], s_s.at[0], r_s.at[0], dev_a(rem(a64 + k, 64)))
        return 0

    lax.fori_loop(1, 64, scalars_a, 0)
    buf_s[a64] = sc[0]

    for c in range(2):
        cols = slice(c * HALF, (c + 1) * HALF)
        send(acc_s.at[other, cols], buf_r.at[1, :, cols], s_rs.at[c], r_rs.at[c], mate)

    def share(t):
        @pl.when(t >= total_steps - STEPS)
        def _share():
            chunk, cols = rem(t, STEPS), columns(t)
            send(acc_k.at[other, cols], buf_r.at[0, :, cols], s_r.at[chunk], r_r.at[chunk], mate)

    def last_kernel(i, _):
        t = 2 * pairs + 1 + 2 * i
        product(0, acc_k, t, odd)
        share(t)
        product(0, acc_k, t + 1, even)
        share(t + 1)
        return 0

    lax.fori_loop(0, LAG // 2, last_kernel, 0)
    product(0, acc_k, total_steps - 1, odd)
    share(jnp.int32(total_steps - 1))

    whole(buf_s.at[0:63], r_s.at[0])
    sc[1] = jnp.sum(buf_s[...], axis=0)

    def scalars_b(k, _):
        send(sc.at[1], buf_s2.at[m_b], s_s.at[1], r_s.at[1], dev_b(rem(m_b + k, 8)))
        return 0

    lax.fori_loop(1, 8, scalars_b, 0)
    buf_s2[m_b] = sc[1]

    for c in range(2):
        cols = slice(c * HALF, (c + 1) * HALF)
        whole(buf_r.at[1, :, cols], r_rs.at[c])
        dkz_out[:, cols] = (acc_s[mine, cols] + buf_r[1, :, cols]) * k_slope
    for c in range(STEPS):
        cols = slice(c * TB, (c + 1) * TB)
        whole(buf_r.at[0, :, cols], r_r.at[c])
        kz_out[:, cols] = acc_k[mine, cols] + buf_r[0, :, cols]

    whole(buf_s2.at[0:7], r_s.at[1])
    total = jnp.sum(jnp.sum(buf_s2[...], axis=0), axis=1, keepdims=True) * (0.5 / COLS)
    grad_out[0] = total[0, 0]
    grad_out[1] = total[1, 0]

    whole(buf_ac.at[0:31], s_a1.at[0])
    whole(buf_a.at[0:63], s_a1.at[1])
    whole(st_ac.at[0:31], s_a2.at[3])
    whole(buf_cc.at[0:7], s_b1.at[3])
    whole(st_bc.at[0:7], s_b2.at[3])
    for r in range(ROUNDS):
        whole(st_a.at[r, 0:31], s_a2.at[r])
        whole(buf_c[r].at[0:7], s_b1.at[r])
        whole(st_b.at[r, 0:7], s_b2.at[r])
    whole(buf_s.at[0:63], s_s.at[0])
    whole(buf_s2.at[0:7], s_s.at[1])
    for c in range(2):
        whole(buf_r.at[1, :, c * HALF:(c + 1) * HALF], s_rs.at[c])
    for c in range(STEPS):
        whole(buf_r.at[0, :, c * TB:(c + 1) * TB], s_r.at[c])


def local(coords, probes, solves, alpha, lengthscale, column_pick, plan):
    rate = math.sqrt(5.0) / lengthscale[0]
    cst = jnp.stack([
        rate * (-math.log2(math.e)), rate, rate * rate / 3.0, rate * rate / (3.0 * lengthscale[0])
    ])
    vm = pl.BlockSpec(memory_space=pltpu.VMEM)
    sm = pl.BlockSpec(memory_space=pltpu.SMEM)
    hb = pl.BlockSpec(memory_space=pl.ANY)
    V, dma = pltpu.VMEM, pltpu.SemaphoreType.DMA
    kz, dkz, grad = pl.pallas_call(
        body,
        out_shape=[
            jax.ShapeDtypeStruct((32, COLS), F32),
            jax.ShapeDtypeStruct((32, COLS), F32),
            jax.ShapeDtypeStruct((2,), F32),
        ],
        in_specs=[sm, sm, sm, hb, hb, hb, hb],
        out_specs=[vm, vm, sm],
        scratch_shapes=[
            V((3, COLS), F32), V((1, COLS), F32), V((32, COLS), F32), V((64, COLS), F32),
            V((4, 16, 1, 128), F32),
            V((64, 8, 128), F32), V((32, 1, 128), F32),
            V((ROUNDS, 32, 2, 8, 128), F32), V((32, 4, 128), F32),
            V((ROUNDS, 8, 4, 2, 8, 128), F32), V((8, 4, 4, 128), F32),
            V((8, 4, 2, 8, 128), F32), V((8, 4, 2, 8, 128), F32), V((8, 4, 2, 8, 128), F32),
            V((8, 4, 4, 128), F32),
            V((ROUNDS, 8, 64, 128), F32), V((8, 4, 4, 128), F32),
            V((ROUNDS, 72, HALF), F32), V((8, 4, 4, 128), F32),
            V((64, COLS), F32),
            V((ROUNDS, 160, HALF), BF16), V((ROUNDS, HALF, 8), F32),
            V((RING, 4, HALF, TB), BF16), V((RING, 4, HALF, TB), BF16),
            V((72, COLS), F32), V((72, COLS), F32),
            V((2, 32, COLS), F32),
            V((2, 2, 128), F32), V((64, 2, 128), F32), V((8, 2, 128), F32),
            dma((4,)),
            dma((2,)), dma((2,)),
            dma((4,)), dma((4,)),
            dma((4,)), dma((4,)),
            dma((4,)), dma((4,)),
            dma((STEPS,)), dma((STEPS,)),
            dma((2,)), dma((2,)),
            dma((2,)), dma((2,)),
        ],
        compiler_params=pltpu.CompilerParams(
            collective_id=0, has_side_effects=True, vmem_limit_bytes=63 * 2 ** 20
        ),
    )(plan, column_pick, cst, coords, alpha.reshape(1, COLS), probes, solves)
    return kz, dkz, grad


def solution(mesh):
    placed = (P(None, "blk"), P("pr", "blk"), P(None, "blk"), P("blk"), P(), P(), P())
    return jax.shard_map(
        local,
        mesh=mesh,
        in_specs=placed,
        out_specs=(P("pr", "blk"), P("pr", "blk"), P()),
        check_vma=False,
    )
```

```python
import math
import jax
import jax.numpy as jnp
from jax import lax
from jax.experimental import pallas as pl
from jax.experimental.pallas import tpu as pltpu
from jax.sharding import PartitionSpec as P

F32, BF16 = jnp.float32, jnp.bfloat16
MESH = pl.DeviceIdType.MESH
ROUNDS = 3
COLS = 2048
HALF = 1024
TB = 256
LAG = 15
RING = 8
STRIP = 16
STEPS = COLS // TB


def split(value):
    hi = value.astype(BF16)
    return hi, (value - hi.astype(F32)).astype(BF16)


def tile_terms(xa, xb, ka, k1, k0):
    d2 = None
    for comp in range(3):
        off = xa[:, comp:comp + 1] - xb[comp]
        d2 = off * off if d2 is None else d2 + off * off
    dist = d2 * lax.rsqrt(jnp.maximum(d2, 1e-30))
    decay = jnp.exp2(dist * ka)
    bell = (k0 + dist * k1) * decay
    return bell + d2 * decay, d2 * bell


def whole(ref, sem):
    pltpu.make_async_copy(ref, ref, sem).wait()


def body(
    plan, pick, cst, coords_h, alpha_h, probes_h, solves_h,
    kz_out, dkz_out, grad_out,
    coords, alpha, probes, solves,
    comps, buf_a, buf_ac, st_a, st_ac, buf_b, buf_bc, buf_c0, buf_c1, buf_c2, buf_cc, st_b, st_bc, p32, payc,
    picked, plhs, xat, even, odd, acc_k, acc_s, buf_r, sc, buf_s, buf_s2,
    s_in, s_a1, r_a1, s_a2, r_a2, s_b1, r_b1, s_b2, r_b2, s_r, r_r, s_rs, r_rs, s_s, r_s,
):
    rem, div = lax.rem, lax.div
    buf_c = (buf_c0, buf_c1, buf_c2)
    blk = lax.axis_index("blk")
    half = lax.axis_index("pr")
    core = rem(blk, 2)
    zhi = rem(div(blk, 2), 4)
    x = rem(div(blk, 8), 4)
    y = div(blk, 32)
    m_a = y * 4 + zhi
    m_b = x * 2 + core
    a64 = half * 32 + m_a
    base_a = x * 8 + core
    base_b = y * 32 + zhi * 2

    def dev_a(k):
        m = rem(k, 32)
        return {"blk": div(m, 4) * 32 + rem(m, 4) * 2 + base_a, "pr": div(k, 32)}

    def dev_b(k):
        return {"blk": base_b + div(k, 2) * 8 + rem(k, 2), "pr": half}

    def send(src, dst, ssem, rsem, dev):
        pltpu.make_async_remote_copy(
            src_ref=src, dst_ref=dst, send_sem=ssem, recv_sem=rsem, device_id=dev, device_id_type=MESH
        ).start()

    fetches = [
        pltpu.make_async_copy(src, dst, s_in.at[n])
        for n, (src, dst) in enumerate(
            [(coords_h, coords), (alpha_h, alpha), (probes_h, probes), (solves_h, solves)]
        )
    ]
    for fetch in fetches:
        fetch.start()

    shifts = [plan[r, 0] for r in range(ROUNDS)]
    t_a = [(s // 32) * 4 + (s // 2) % 4 for s in shifts]
    t_b = [((s // 8) % 4) * 2 + s % 2 for s in shifts]

    barrier = pltpu.get_barrier_semaphore()

    def greet_a(k, _):
        pl.semaphore_signal(barrier, inc=1, device_id=dev_a(rem(a64 + k, 64)), device_id_type=MESH)
        return 0

    def greet_b(k, _):
        pl.semaphore_signal(barrier, inc=1, device_id=dev_b(rem(m_b + k, 8)), device_id_type=MESH)
        return 0

    lax.fori_loop(1, 64, greet_a, 0)
    lax.fori_loop(1, 8, greet_b, 0)

    fetches[0].wait()
    fetches[1].wait()
    for g in range(4):
        row = coords[g:g + 1, :] if g < 3 else alpha[...]
        for t in range(16):
            comps[g, t] = row[:, t * 128:(t + 1) * 128]
    fetches[2].wait()
    pl.semaphore_wait(barrier, 70)

    def probe_tile(hh, yy, zz):
        rows = pl.ds(pl.multiple_of(zz * 8, 8), 8)
        return rows, pl.ds(pl.multiple_of(hh * HALF + yy * 128, 128), 128)

    def spread_comps(k, _):
        m = rem(m_a + k, 32)
        send(comps.at[rem(m, 4), half * 8 + div(m, 4)], buf_ac.at[m_a], s_a1.at[0], r_a1.at[0], dev_a(half * 32 + m))
        return 0

    def spread_probes(k, _):
        d = rem(a64 + k, 64)
        m = rem(d, 32)
        rows, cols = probe_tile(div(d, 32), div(m, 4), rem(m, 4))
        send(probes.at[rows, cols], buf_a.at[a64], s_a1.at[1], r_a1.at[1], dev_a(d))
        return 0

    lax.fori_loop(1, 32, spread_comps, 0)
    lax.fori_loop(1, 64, spread_probes, 0)
    buf_ac[m_a] = comps[zhi, half * 8 + y]
    rows, cols = probe_tile(half, y, zhi)
    buf_a[a64] = probes[rows, cols]

    other = pl.ds(pl.multiple_of((1 - half) * 32, 32), 32)
    mine = pl.ds(pl.multiple_of(half * 32, 32), 32)
    mate = {"blk": blk, "pr": 1 - half}

    fetches[3].wait()
    for j in range(64):
        picked[j:j + 1, :] = solves[pl.ds(pick[j], 1), :]
    acc_k[...] = jnp.zeros_like(acc_k)
    acc_s[...] = jnp.zeros_like(acc_s)
    noise = jnp.sum(picked[mine, :] * probes[...], axis=0, keepdims=True)
    own = alpha[...]
    noise = 0.5 * own * own - noise * (1.0 / 64.0)

    def fold(row):
        total = row[:, 0:128]
        for t in range(1, 16):
            total = total + row[:, t * 128:(t + 1) * 128]
        return total

    sc[0, 0:1, :] = fold(noise)
    whole(buf_ac.at[0:31], r_a1.at[0])

    def select_ac(k, _):
        i = rem(m_a + k, 32)
        for r in range(ROUNDS):
            st_ac[i, r:r + 1, :] = buf_ac[i ^ t_a[r]]
        st_ac[i, 3:4, :] = jnp.zeros((1, 128), F32)
        send(st_ac.at[i], buf_bc.at[y, zhi], s_a2.at[3], r_a2.at[3], dev_a(half * 32 + i))
        return 0

    lax.fori_loop(1, 32, select_ac, 0)
    for r in range(ROUNDS):
        buf_bc[y, zhi, r:r + 1, :] = buf_ac[m_a ^ t_a[r]]
    buf_bc[y, zhi, 3:4, :] = jnp.zeros((1, 128), F32)

    def select_a(r):
        def one(k, _):
            i = rem(m_a + k, 32)
            j = i ^ t_a[r]
            st_a[r, i, 0] = buf_a[j]
            st_a[r, i, 1] = buf_a[32 + j]
            send(st_a.at[r, i], buf_b.at[r, y, zhi], s_a2.at[r], r_a2.at[r], dev_a(half * 32 + i))
            return 0

        lax.fori_loop(1, 32, one, 0)
        j = m_a ^ t_a[r]
        buf_b[r, y, zhi, 0] = buf_a[j]
        buf_b[r, y, zhi, 1] = buf_a[32 + j]

    def spread_b(r):
        whole(st_a.at[r, 0:31], r_a2.at[r])

        def one(k, _):
            d = rem(m_b + k, 8)
            send(buf_b.at[r, d], buf_c[r].at[m_b], s_b1.at[r], r_b1.at[r], dev_b(d))
            return 0

        lax.fori_loop(1, 8, one, 0)
        buf_c[r][m_b] = buf_b[r, m_b]

    def select_b(r):
        whole(buf_c[r].at[0:7], r_b1.at[r])
        cols = pl.ds(pl.multiple_of(m_b * 128, 128), 128)

        def one(k, _):
            d = rem(m_b + k, 8)
            j = d ^ t_b[r]
            for hh in range(2):
                for g in range(4):
                    lo = (hh * 4 + g) * 8
                    st_b[r, d, lo:lo + 8, :] = buf_c[r][j, g, hh]
            send(st_b.at[r, d], p32.at[r, 0:64, cols], s_b2.at[r], r_b2.at[r], dev_b(d))
            return 0

        lax.fori_loop(1, 8, one, 0)
        j = m_b ^ t_b[r]
        for hh in range(2):
            for g in range(4):
                lo = (hh * 4 + g) * 8
                p32[r, lo:lo + 8, cols] = buf_c[r][j, g, hh]

    whole(buf_a.at[0:63], r_a1.at[1])
    for r in range(ROUNDS):
        select_a(r)
    whole(st_ac.at[0:31], r_a2.at[3])

    def spread_bc(k, _):
        d = rem(m_b + k, 8)
        send(buf_bc.at[d], buf_cc.at[m_b], s_b1.at[3], r_b1.at[3], dev_b(d))
        return 0

    lax.fori_loop(1, 8, spread_bc, 0)
    buf_cc[m_b] = buf_bc[m_b]
    whole(buf_cc.at[0:7], r_b1.at[3])

    def select_bc(k, _):
        d = rem(m_b + k, 8)
        for r in range(ROUNDS):
            for g in range(4):
                st_bc[d, g, r:r + 1, :] = buf_cc[d ^ t_b[r], g, r:r + 1, :]
        for g in range(4):
            st_bc[d, g, 3:4, :] = jnp.zeros((1, 128), F32)
        send(st_bc.at[d], payc.at[m_b], s_b2.at[3], r_b2.at[3], dev_b(d))
        return 0

    lax.fori_loop(1, 8, select_bc, 0)
    for r in range(ROUNDS):
        for g in range(4):
            payc[m_b, g, r:r + 1, :] = buf_cc[m_b ^ t_b[r], g, r:r + 1, :]

    whole(st_bc.at[0:7], r_b2.at[3])
    for r in range(ROUNDS):
        for t in range(8):
            for g in range(4):
                p32[r, 64 + g:65 + g, t * 128:(t + 1) * 128] = payc[t, g, r:r + 1, :]
        p32[r, 68:72, :] = jnp.zeros((4, HALF), F32)
        xat[r] = jnp.transpose(p32[r, 64:72, :])

    ka, k1, k0, k_kernel, k_slope = cst[0], cst[1], cst[2], cst[3], cst[4]

    def columns(t):
        return pl.ds(pl.multiple_of(rem(t, STEPS) * TB, TB), TB)

    def tiles(t, ring):
        r, slot = div(t, STEPS), rem(div(t, 2), RING)
        xb = [coords[c:c + 1, columns(t)] for c in range(3)]
        for st in range(0, HALF, STRIP):
            kern, slope = tile_terms(xat[r, st:st + STRIP, :], xb, ka, k1, k0)
            ring[slot, 0, st:st + STRIP, :], ring[slot, 1, st:st + STRIP, :] = split(kern)
            ring[slot, 2, st:st + STRIP, :], ring[slot, 3, st:st + STRIP, :] = split(slope)

    def product(n, acc, t, ring):
        r, slot = div(t, STEPS), rem(div(t, 2), RING)
        one = jnp.dot(plhs[r], ring[slot, 2 * n], preferred_element_type=F32)
        two = jnp.dot(plhs[r, 0:80, :], ring[slot, 2 * n + 1], preferred_element_type=F32)
        acc[:, columns(t)] += one[:72] + one[80:152] + two[:72]

    def products(t, ring):
        product(0, acc_k, t, ring)
        product(1, acc_s, t, ring)

    def prepare(r):
        whole(st_b.at[r, 0:7], r_b2.at[r])
        hi, lo = split(jnp.concatenate([p32[r], jnp.zeros((8, HALF), F32)], 0))
        plhs[r, 0:80, :] = hi
        plhs[r, 80:160, :] = lo

    def first(i, _):
        tiles(2 * i, even)
        tiles(2 * i + 1, odd)

        @pl.when(i == 0)
        def _hook_0():
            spread_b(0)

        @pl.when(i == 2)
        def _hook_2():
            spread_b(1)
            select_b(0)

        @pl.when(i == 4)
        def _hook_4():
            spread_b(2)
            select_b(1)

        @pl.when(i == 6)
        def _hook_6():
            select_b(2)

        return 0

    lax.fori_loop(0, LAG // 2, first, 0)
    tiles(LAG - 1, even)

    prepare(0)

    def second(i, _):
        tiles(2 * i + LAG, odd)
        products(2 * i, even)
        tiles(2 * i + LAG + 1, even)
        products(2 * i + 1, odd)
        return 0

    total_steps = ROUNDS * STEPS
    pairs = (total_steps - LAG) // 2
    lax.fori_loop(0, 2, second, 0)
    prepare(1)

    def third(i, _):
        tiles(2 * i + LAG, odd)
        products(2 * i, even)
        product(1, acc_s, 2 * i + 4, even)
        tiles(2 * i + LAG + 1, even)
        products(2 * i + 1, odd)
        product(1, acc_s, 2 * i + 5, odd)
        return 0

    lax.fori_loop(2, pairs, third, 0)
    tiles(total_steps - 1, odd)
    prepare(2)

    def last_slope(i, _):
        product(1, acc_s, 2 * i, even)
        product(1, acc_s, 2 * i + 1, odd)
        return 0

    lax.fori_loop(pairs + 2, total_steps // 2, last_slope, 0)

    slope = acc_s[67:68, :] * own - jnp.sum(picked[...] * acc_s[0:64, :], axis=0, keepdims=True) * (1.0 / 64.0)
    sc[0, 1:2, :] = fold(slope) * k_slope

    def scalars_a(k, _):
        send(sc.at[0], buf_s.at[a64], s_s.at[0], r_s.at[0], dev_a(rem(a64 + k, 64)))
        return 0

    lax.fori_loop(1, 64, scalars_a, 0)
    buf_s[a64] = sc[0]

    for c in range(2):
        cols = slice(c * HALF, (c + 1) * HALF)
        send(acc_s.at[other, cols], buf_r.at[1, :, cols], s_rs.at[c], r_rs.at[c], mate)

    def share(t):
        @pl.when(t >= total_steps - STEPS)
        def _share():
            chunk, cols = rem(t, STEPS), columns(t)
            send(acc_k.at[other, cols], buf_r.at[0, :, cols], s_r.at[chunk], r_r.at[chunk], mate)

    def last_kernel(i, _):
        product(0, acc_k, 2 * i, even)
        share(2 * i)
        product(0, acc_k, 2 * i + 1, odd)
        share(2 * i + 1)
        return 0

    lax.fori_loop(pairs, total_steps // 2, last_kernel, 0)

    whole(buf_s.at[0:63], r_s.at[0])
    sc[1] = jnp.sum(buf_s[...], axis=0)

    def scalars_b(k, _):
        send(sc.at[1], buf_s2.at[m_b], s_s.at[1], r_s.at[1], dev_b(rem(m_b + k, 8)))
        return 0

    lax.fori_loop(1, 8, scalars_b, 0)
    buf_s2[m_b] = sc[1]

    for c in range(2):
        cols = slice(c * HALF, (c + 1) * HALF)
        whole(buf_r.at[1, :, cols], r_rs.at[c])
        dkz_out[:, cols] = (acc_s[mine, cols] + buf_r[1, :, cols]) * k_slope
    for c in range(STEPS):
        cols = slice(c * TB, (c + 1) * TB)
        whole(buf_r.at[0, :, cols], r_r.at[c])
        kz_out[:, cols] = (acc_k[mine, cols] + buf_r[0, :, cols]) * k_kernel

    whole(buf_s2.at[0:7], r_s.at[1])
    total = jnp.sum(jnp.sum(buf_s2[...], axis=0), axis=1, keepdims=True) * (0.5 / COLS)
    grad_out[0] = total[0, 0]
    grad_out[1] = total[1, 0]

    whole(buf_ac.at[0:31], s_a1.at[0])
    whole(buf_a.at[0:63], s_a1.at[1])
    whole(st_ac.at[0:31], s_a2.at[3])
    whole(buf_cc.at[0:7], s_b1.at[3])
    whole(st_bc.at[0:7], s_b2.at[3])
    for r in range(ROUNDS):
        whole(st_a.at[r, 0:31], s_a2.at[r])
        whole(buf_c[r].at[0:7], s_b1.at[r])
        whole(st_b.at[r, 0:7], s_b2.at[r])
    whole(buf_s.at[0:63], s_s.at[0])
    whole(buf_s2.at[0:7], s_s.at[1])
    for c in range(2):
        whole(buf_r.at[1, :, c * HALF:(c + 1) * HALF], s_rs.at[c])
    for c in range(STEPS):
        whole(buf_r.at[0, :, c * TB:(c + 1) * TB], s_r.at[c])


def local(coords, probes, solves, alpha, lengthscale, column_pick, plan):
    rate = math.sqrt(5.0) / lengthscale[0]
    square = rate * rate / 3.0
    cst = jnp.stack([
        rate * (-math.log2(math.e)), rate / square, 1.0 / square, square,
        square * (square / lengthscale[0]),
    ])
    vm = pl.BlockSpec(memory_space=pltpu.VMEM)
    sm = pl.BlockSpec(memory_space=pltpu.SMEM)
    hb = pl.BlockSpec(memory_space=pl.ANY)
    V, dma = pltpu.VMEM, pltpu.SemaphoreType.DMA
    kz, dkz, grad = pl.pallas_call(
        body,
        out_shape=[
            jax.ShapeDtypeStruct((32, COLS), F32),
            jax.ShapeDtypeStruct((32, COLS), F32),
            jax.ShapeDtypeStruct((2,), F32),
        ],
        in_specs=[sm, sm, sm, hb, hb, hb, hb],
        out_specs=[vm, vm, sm],
        scratch_shapes=[
            V((3, COLS), F32), V((1, COLS), F32), V((32, COLS), F32), V((64, COLS), F32),
            V((4, 16, 1, 128), F32),
            V((64, 8, 128), F32), V((32, 1, 128), F32),
            V((ROUNDS, 32, 2, 8, 128), F32), V((32, 4, 128), F32),
            V((ROUNDS, 8, 4, 2, 8, 128), F32), V((8, 4, 4, 128), F32),
            V((8, 4, 2, 8, 128), F32), V((8, 4, 2, 8, 128), F32), V((8, 4, 2, 8, 128), F32),
            V((8, 4, 4, 128), F32),
            V((ROUNDS, 8, 64, 128), F32), V((8, 4, 4, 128), F32),
            V((ROUNDS, 72, HALF), F32), V((8, 4, 4, 128), F32),
            V((64, COLS), F32),
            V((ROUNDS, 160, HALF), BF16), V((ROUNDS, HALF, 8), F32),
            V((RING, 4, HALF, TB), BF16), V((RING, 4, HALF, TB), BF16),
            V((72, COLS), F32), V((72, COLS), F32),
            V((2, 32, COLS), F32),
            V((2, 2, 128), F32), V((64, 2, 128), F32), V((8, 2, 128), F32),
            dma((4,)),
            dma((2,)), dma((2,)),
            dma((4,)), dma((4,)),
            dma((4,)), dma((4,)),
            dma((4,)), dma((4,)),
            dma((STEPS,)), dma((STEPS,)),
            dma((2,)), dma((2,)),
            dma((2,)), dma((2,)),
        ],
        compiler_params=pltpu.CompilerParams(
            collective_id=0, has_side_effects=True, vmem_limit_bytes=63 * 2 ** 20
        ),
    )(plan, column_pick, cst, coords, alpha.reshape(1, COLS), probes, solves)
    return kz, dkz, grad


def solution(mesh):
    placed = (P(None, "blk"), P("pr", "blk"), P(None, "blk"), P("blk"), P(), P(), P())
    return jax.shard_map(
        local,
        mesh=mesh,
        in_specs=placed,
        out_specs=(P("pr", "blk"), P("pr", "blk"), P()),
        check_vma=False,
    )
```
